128 devices in a mesh: leaf: 32 (over x, z, core), sub: 4 (over y).
Axes of the slice: x: 4, y: 4, z: 4, core: 2. Of those that a mesh axis runs over, the one named last changes fastest.
Arguments:
- rhs: float32 [64, 1048576], P(None, ('leaf', 'sub')), may hold values from -6 to 6
- iterate: float32 [64, 1048576], P(None, ('leaf', 'sub')), may hold values from -6 to 6
- residual: float32 [64, 1048576], P(None, ('leaf', 'sub')), may hold values from -66 to 66
- direction: float32 [64, 1048576], P(None, ('leaf', 'sub')), may hold values from -66 to 66
- points: float32 [8, 1048576], P(None, ('leaf', 'sub')), may hold values from -1.4 to 2.4
- skeletons: float32 [8, 262144], P(None, ('leaf', 'sub')), may hold values from -1.4 to 2.4
- leaf_basis: float32 [64, 1048576], P(None, ('leaf', 'sub')), may hold values from -0.75 to 0.75
- device_basis: float32 [64, 262144], P(None, ('leaf', 'sub')), may hold values from -0.375 to 0.375
- transfer: float32 [126, 64, 128], replicated, may hold values from -0.625 to 0.625
- node_coords: float32 [8, 8064], replicated, may hold values from -1.4 to 2.4
- near_list: int32 [4096, 8], P(('leaf', 'sub')), may hold values from -1 to 63, as said below
- far_list: int32 [4096, 8], P(('leaf', 'sub')), may hold values from -1 to 63, as said below
Outputs:
- new_iterate: float32 [64, 1048576], P(None, ('leaf', 'sub'))
- new_residual: float32 [64, 1048576], P(None, ('leaf', 'sub'))
- new_direction: float32 [64, 1048576], P(None, ('leaf', 'sub'))
- true_residual: float32 [64, 1048576], P(None, ('leaf', 'sub'))
The draws below stay inside these ranges and needn't reach their ends.
Inputs may be any that keep to these rules, and one draw needn't show every extreme that they name: `near_list`: live entries of a row come first and entry 0 is the leaf itself; a row names no source twice and none that the same leaf's far_list row names; a device block holds at most 192 live entries. `far_list`: live entries of a row come first; at least half of a row is live.
All inputs are finite; a program needn't handle non-finite values.
Results may differ from the reference program's by a relative error of at most 0.0003.
Values sent between devices are 32-bit elements; how exact they have to be, the bound alone decides.
A program may use at most 256 MiB of HBM per device.

```python
import math
import jax
import jax.numpy as jnp
from jax import lax

DIM = 8
LEAF = 256
RANK = 64
NRHS = 64
LEAF_DEV = 32
NEAR = 8
FAR = 8
NEAR_LIVE = 192
LEAVES = 4096
POINTS = 1048576
NODES = 126
N_LEAF = 32
N_SUB = 4
DEVICES = 128


def vector_field(key):
    base = jnp.clip(jax.random.normal(jax.random.fold_in(key, 21), (NRHS, DEVICES, LEAF_DEV * LEAF)), -6.0, 6.0)
    column_scale = 0.3 * jnp.exp(jnp.log(10.0) * jax.random.uniform(jax.random.fold_in(key, 22), (NRHS, 1, 1)))
    device_scale = 0.6 * jnp.exp(jnp.log(3.0) * jnp.arange(DEVICES, dtype=jnp.float32) / (DEVICES - 1))
    values = base * column_scale * device_scale[None, :, None]
    return values.reshape(NRHS, POINTS)


def draw_residual(key, part):
    key = jax.random.fold_in(key, 5)
    return vector_field(key)


def draw_direction(key, part):
    key = jax.random.fold_in(key, 15)
    return vector_field(key)


def leaf_centers(key):
    return jax.random.uniform(jax.random.fold_in(key, 40), (DIM, LEAVES))


def draw_points(key, part):
    centers = leaf_centers(key)
    key = jax.random.fold_in(key, 7)
    spread = 0.35 * jnp.clip(jax.random.normal(key, (DIM, POINTS)), -4.0, 4.0)
    return jnp.repeat(centers, LEAF, axis=1) + spread


def draw_skeletons(key, part):
    centers = leaf_centers(key)
    key = jax.random.fold_in(key, 8)
    spread = 0.35 * jnp.clip(jax.random.normal(key, (DIM, LEAVES * RANK)), -4.0, 4.0)
    return jnp.repeat(centers, RANK, axis=1) + spread


def draw_node_coords(key, part):
    key = jax.random.fold_in(key, 9)
    centers = jax.random.uniform(jax.random.fold_in(key, 1), (DIM, NODES))
    spread = 0.35 * jnp.clip(jax.random.normal(jax.random.fold_in(key, 2), (DIM, NODES * RANK)), -4.0, 4.0)
    return jnp.repeat(centers, RANK, axis=1) + spread


def interaction_lists(key):
    sources = 2 * LEAF_DEV
    column = jnp.arange(sources, dtype=jnp.int32)[None, :]
    own_leaf = (jnp.arange(LEAVES, dtype=jnp.int32) % LEAF_DEV)[:, None]
    scores = jax.random.randint(jax.random.fold_in(key, 51), (LEAVES, sources), 0, 1048576) * sources + column
    scores = jnp.where(column == own_leaf, -1, scores)
    order = jnp.argsort(scores, axis=1, stable=True).astype(jnp.int32)
    slot_near = jnp.arange(NEAR, dtype=jnp.int32)[None, :]
    counts = jax.random.randint(jax.random.fold_in(key, 52), (DEVICES, LEAF_DEV), 1, NEAR + 1)
    heavy = jax.random.randint(jax.random.fold_in(key, 53), (), 0, DEVICES)
    counts = jnp.where(jnp.arange(DEVICES, dtype=jnp.int32)[:, None] == heavy, NEAR, counts)
    extras = counts - 1
    before = (jnp.cumsum(extras, axis=1) - extras).reshape(LEAVES, 1)
    live = (slot_near == 0) | (slot_near < counts.reshape(LEAVES, 1)) & (before + slot_near - 1 < NEAR_LIVE - LEAF_DEV)
    near_rows = jnp.where(live, order[:, :NEAR], -1)
    far_counts = jax.random.randint(jax.random.fold_in(key, 54), (LEAVES, 1), (FAR + 1) // 2, FAR + 1)
    slot_far = jnp.arange(FAR, dtype=jnp.int32)[None, :]
    far_rows = jnp.where(slot_far < far_counts, order[:, NEAR:NEAR + FAR], -1)
    return (near_rows.astype(jnp.int32), far_rows.astype(jnp.int32))


def draw_near_list(key, part):
    near_rows, far_rows = interaction_lists(key)
    return near_rows


def draw_far_list(key, part):
    near_rows, far_rows = interaction_lists(key)
    return far_rows


def block_levels(stream_key, shape, pieces, least, top_value):
    gain = 1.0
    for dim, shards_of in pieces:
        draws = jax.random.uniform(jax.random.fold_in(jax.random.fold_in(stream_key, 6), dim), (shards_of,), jnp.float32, least / len(pieces), top_value / len(pieces))
        gain = gain * jnp.repeat(jnp.exp(draws), shape[dim] // shards_of).reshape((-1,) + (1,) * (len(shape) - 1 - dim))
    return gain


def centred(own_key, shape, scale, reach, pieces=(), kind=jnp.bfloat16):
    gain = block_levels(own_key, shape, pieces, -0.22, 0.18) if pieces else 1.0
    drawn = jax.random.normal(own_key, shape, jnp.float32) * scale * gain
    return jnp.minimum(jnp.maximum(drawn, -reach), reach).astype(kind)


def setup_inputs(seed: int = 0) -> dict:
    streams_of = jax.random.split(jax.random.key(seed), 13)
    rhs = centred(streams_of[0], (NRHS, POINTS), 1.0, 6.0, ((1, 128),), jnp.float32)
    iterate = centred(streams_of[1], (NRHS, POINTS), 1.0, 6.0, ((1, 128),), jnp.float32)
    residual = draw_residual(jax.random.fold_in(streams_of[12], 71), 0)
    direction = draw_direction(jax.random.fold_in(streams_of[12], 71), 0)
    points = draw_points(jax.random.fold_in(streams_of[12], 71), 0)
    skeletons = draw_skeletons(jax.random.fold_in(streams_of[12], 71), 0)
    leaf_basis = centred(streams_of[6], (RANK, POINTS), RANK ** -0.5, 0.75, ((1, 128),), jnp.float32)
    device_basis = centred(streams_of[7], (RANK, LEAVES * RANK), LEAF ** -0.5, 0.375, ((1, 128),), jnp.float32)
    transfer = centred(streams_of[8], (NODES, RANK, 2 * RANK), (RANK * 3 // 2) ** -0.5, 0.625, (), jnp.float32)
    node_coords = draw_node_coords(jax.random.fold_in(streams_of[12], 71), 0)
    near_list = draw_near_list(jax.random.fold_in(streams_of[12], 71), 0)
    far_list = draw_far_list(jax.random.fold_in(streams_of[12], 71), 0)
    return {"rhs": rhs, "iterate": iterate, "residual": residual, "direction": direction, "points": points, "skeletons": skeletons, "leaf_basis": leaf_basis, "device_basis": device_basis, "transfer": transfer, "node_coords": node_coords, "near_list": near_list, "far_list": far_list}


noise_level = 1.0
amplitude = 0.1
length_scale = 1.0
highest = lax.Precision.HIGHEST

def matern(first_pts, second_pts):
    cross = jnp.einsum('bdm,bdn->bmn', first_pts, second_pts, precision=highest)
    first_sq = lax.optimization_barrier(jnp.sum(first_pts * first_pts, axis=1))
    second_sq = lax.optimization_barrier(jnp.sum(second_pts * second_pts, axis=1))
    dist_sq = first_sq[:, :, None] + second_sq[:, None, :] - 2.0 * cross
    scaled = math.sqrt(3.0) / length_scale * jnp.sqrt(jnp.maximum(dist_sq, 0.0))
    return amplitude * (1.0 + scaled) * jnp.exp(-scaled)

def near_block(points_tab, vector_tab, targets, sources, weights):
    target_pts = jnp.take(points_tab, targets, axis=0)
    source_pts = jnp.take(points_tab, sources, axis=0)
    kernel = matern(source_pts, target_pts)
    source_vec = jnp.take(vector_tab, sources, axis=1)
    terms = jnp.einsum('nbq,bqp->bnp', source_vec, kernel, precision=highest)
    return terms * weights[:, None, None]

def near_terms(points_tab, vector_tab, targets, sources, weights):
    number = targets.shape[0]
    stride = math.gcd(number, 32)

    def one_block(packed):
        return near_block(points_tab, vector_tab, packed[0], packed[1], packed[2])
    shaped = (targets.reshape(number // stride, stride), sources.reshape(number // stride, stride), weights.reshape(number // stride, stride))
    result = lax.map(one_block, shaped)
    return result.reshape(number, vector_tab.shape[0], vector_tab.shape[2])

def far_terms(skel_tab, weight_tab, far_rows):
    leaves, slots = far_rows.shape
    targets = jnp.repeat(jnp.arange(leaves, dtype=jnp.int32), slots)
    flat = far_rows.reshape(-1)
    sources = jnp.maximum(flat, 0)
    weights = (flat >= 0).astype(weight_tab.dtype)
    kernel = matern(jnp.take(skel_tab, targets, axis=0), jnp.take(skel_tab, sources, axis=0))
    terms = jnp.einsum('bij,bjn->bin', kernel, jnp.take(weight_tab, sources, axis=0), precision=highest)
    terms = terms * weights[:, None, None]
    return terms.reshape(leaves, slots, terms.shape[1], terms.shape[2]).sum(axis=1)

def pair_flip(values):
    number = values.shape[0]
    return values.reshape((number // 2, 2) + values.shape[1:])[:, ::-1].reshape(values.shape)

def tree_all(base, transfer, node_coords, heights):
    device_total, skel_rank, columns = base.shape
    coords = node_coords.reshape(node_coords.shape[0], -1, skel_rank).transpose(1, 0, 2)
    current = base
    matrices = [None]
    coupled = [None]
    for height in range(1, heights):
        nodes_here = device_total >> height
        offset = device_total - 2 * nodes_here
        matrix = transfer[offset:offset + nodes_here]
        stacked = current.reshape(nodes_here, 2 * skel_rank, columns)
        current = jnp.einsum('nrk,nkm->nrm', matrix, stacked, precision=highest)
        own_coords = coords[offset:offset + nodes_here]
        kernel = matern(own_coords, pair_flip(own_coords))
        coupled.append(jnp.einsum('nij,njm->nim', kernel, pair_flip(current), precision=highest))
        matrices.append(matrix)
    downward = coupled[heights - 1]
    for height in range(heights - 1, 0, -1):
        nodes_here = device_total >> height
        halves = matrices[height].reshape(nodes_here, skel_rank, 2, skel_rank)
        child = jnp.einsum('nrhk,nrm->nhkm', halves, downward, precision=highest)
        downward = child.reshape(2 * nodes_here, skel_rank, columns)
        if height > 1:
            downward = downward + coupled[height - 1]
    return downward

def to_tree(values):
    return values.reshape((N_LEAF, N_SUB) + values.shape[1:]).swapaxes(0, 1).reshape(values.shape)

def from_tree(values):
    return values.reshape((N_SUB, N_LEAF) + values.shape[1:]).swapaxes(0, 1).reshape(values.shape)

def h2_apply(vector, points, skeletons, leaf_basis, device_basis, transfer, node_coords, near_list, far_list):
    columns = vector.shape[0]
    vec4 = vector.reshape(columns, DEVICES, LEAF_DEV, LEAF).transpose(1, 0, 2, 3)
    pts4 = points.reshape(DIM, DEVICES, LEAF_DEV, LEAF).transpose(1, 2, 0, 3)
    skel4 = skeletons.reshape(DIM, DEVICES, LEAF_DEV, RANK).transpose(1, 2, 0, 3)
    basis4 = leaf_basis.reshape(RANK, DEVICES, LEAF_DEV, LEAF).transpose(1, 0, 2, 3)
    block_basis = device_basis.reshape(RANK, DEVICES, LEAF_DEV * RANK).transpose(1, 0, 2)
    leaf_w = jnp.einsum('grlp,gnlp->glrn', basis4, vec4, precision=highest)
    dev_w = jnp.einsum('grk,gkn->grn', block_basis, leaf_w.reshape(DEVICES, LEAF_DEV * RANK, columns), precision=highest)
    heights = DEVICES.bit_length() - 1
    bottom = from_tree(tree_all(to_tree(dev_w), transfer, node_coords, heights))
    near4 = near_list.reshape(DEVICES, LEAF_DEV, NEAR)
    far4 = far_list.reshape(DEVICES, LEAF_DEV, FAR)

    def one_device(device):
        partner = device ^ N_SUB
        points_tab = jnp.concatenate([pts4[device], pts4[partner]], axis=0)
        vector_tab = jnp.concatenate([vec4[device], vec4[partner]], axis=1)
        skel_tab = jnp.concatenate([skel4[device], skel4[partner]], axis=0)
        weight_tab = jnp.concatenate([leaf_w[device], leaf_w[partner]], axis=0)
        flat = near4[device].reshape(-1)
        targets = jnp.repeat(jnp.arange(LEAF_DEV, dtype=jnp.int32), NEAR)
        terms = near_terms(points_tab, vector_tab, targets, jnp.maximum(flat, 0), (flat >= 0).astype(vector.dtype))
        near_part = terms.reshape(LEAF_DEV, NEAR, columns, LEAF).sum(axis=1)
        z_leaf = jnp.dot(block_basis[device].T, bottom[device], precision=highest).reshape(LEAF_DEV, RANK, columns)
        z_leaf = z_leaf + far_terms(skel_tab, weight_tab, far4[device])
        far_part = jnp.einsum('rlp,lrn->lnp', basis4[device], z_leaf, precision=highest)
        return near_part + far_part
    mixed = lax.map(one_device, jnp.arange(DEVICES, dtype=jnp.int32))
    return noise_level * vector + mixed.transpose(2, 0, 1, 3).reshape(columns, -1)

def reference(rhs, iterate, residual, direction, points, skeletons, leaf_basis, device_basis, transfer, node_coords, near_list, far_list):

    def operator(vector):
        return h2_apply(vector, points, skeletons, leaf_basis, device_basis, transfer, node_coords, near_list, far_list)
    norm_old = lax.optimization_barrier(jnp.sum(residual * residual, axis=1))
    image = operator(direction)
    curvature = lax.optimization_barrier(jnp.sum(direction * image, axis=1))
    alpha = norm_old / curvature
    new_iterate = iterate + alpha[:, None] * direction
    new_residual = residual - alpha[:, None] * image
    norm_new = lax.optimization_barrier(jnp.sum(new_residual * new_residual, axis=1))
    new_direction = new_residual + (norm_new / norm_old)[:, None] * direction
    true_residual = rhs - operator(new_iterate)
    return (new_iterate, new_residual, new_direction, true_residual)
```

```python
import functools
import math

import jax
import jax.numpy as jnp
from jax import lax
from jax.experimental import pallas as pl
from jax.experimental.pallas import tpu as pltpu
from jax.sharding import PartitionSpec as P

MESH = pl.DeviceIdType.MESH
f32, bf16 = jnp.float32, jnp.bfloat16
noise_level = 1.0
amplitude = 0.1
length_scale = 1.0
LN2 = math.log(2.0)
COORD = math.sqrt(3.0) / length_scale / LN2
LEAVES, LEAF, RANK, COLS = 32, 256, 64, 64
SLOTS, BUFS, AHEAD = 200, 8, 4
CORE = (1,)
RINGS = ((2, 4, 6), (8, 16, 24), (32, 64, 96))


def dot(a, b):
    return lax.dot_general(a, b, (((1,), (0,)), ((), ())), preferred_element_type=f32)


def dot_nt(a, b):
    return lax.dot_general(a, b, (((1,), (1,)), ((), ())), preferred_element_type=f32)


def split(a):
    hi = a.astype(bf16)
    return hi, (a - hi.astype(f32)).astype(bf16)


def dot3(a, b):
    ah, al = split(a)
    bh, bl = split(b)
    return dot(ah, bh) + (dot(ah, bl) + dot(al, bh))


def kern(u):
    t = jnp.maximum(u, 1e-12)
    s = t * lax.rsqrt(t)
    return (amplitude + (amplitude * LN2) * s) * jnp.exp2(-s)


def pieces(a):
    one = a.astype(bf16).astype(f32)
    rest = a - one
    two = rest.astype(bf16).astype(f32)
    three = (rest - two).astype(bf16).astype(f32)
    return one, two, three


def features(coords):
    a = coords * COORD
    a1, a2, a3 = pieces(a)
    n1, n2, n3 = pieces(jnp.sum(a * a, axis=0, keepdims=True))
    row = lax.broadcasted_iota(jnp.int32, a.shape, 0)
    norm = jnp.where((row == 0) | (row == 3), n1, jnp.where((row == 1) | (row == 4), n2, n3))
    zero = jnp.zeros_like(a)
    src_norm = jnp.where(row < 3, norm, jnp.where(row < 6, 1.0, 0.0))
    tgt_norm = jnp.where(row < 3, 1.0, jnp.where(row < 6, norm, 0.0))
    s1, s2, s3 = -2.0 * a1, -2.0 * a2, -2.0 * a3
    source = jnp.concatenate([s1, s1, s2, s2, s1, s3, src_norm, zero], axis=0)
    target = jnp.concatenate([a1, a2, a1, a2, a3, a1, tgt_norm, zero], axis=0)
    return source, target


def tree_position():
    return lax.axis_index("sub") * 32 + lax.axis_index("leaf")


def device_at(q):
    return (lax.rem(q, 32), lax.div(q, 32))


def greet(masks):
    q = tree_position()
    barrier = pltpu.get_barrier_semaphore()
    for mask in masks:
        pl.semaphore_signal(barrier, inc=1, device_id=device_at(q ^ mask), device_id_type=MESH)


def await_greetings(masks):
    pl.semaphore_wait(pltpu.get_barrier_semaphore(), len(masks))


def exchange(buf, number, masks, send, recv):
    q = tree_position()
    return [
        pltpu.make_async_remote_copy(
            buf.at[number, 0],
            buf.at[number, i + 1],
            send.at[number, i],
            recv.at[number, i],
            device_id=device_at(q ^ mask),
            device_id_type=MESH,
        )
        for i, mask in enumerate(masks)
    ]


def climb_kernel(
    d, x, lb, db, transfer, nc, pts, sk,
    z0, w_own, dp, xp, wp, ptp, skp,
    mats, kmask, buf, mat_sem, far_send, far_recv, send, recv,
):
    q = tree_position()
    every = CORE + sum(RINGS, ())
    greet(every)
    spots = []
    for c in range(1, 7):
        base = 128 - 2 * (128 >> c)
        node = lax.shift_right_logical(q, c)
        if c % 2:
            spots.append((base + node, 1, (c - 1) // 2 * 3))
        else:
            spots.append((base + (node & -2), 2, (c - 2) // 2 * 3 + 1))
    loads = [
        pltpu.make_async_copy(transfer.at[pl.ds(at, n)], mats.at[pl.ds(slot, n)], mat_sem.at[i])
        for i, (at, n, slot) in enumerate(spots)
    ]
    for load in loads:
        load.start()
    await_greetings(every)
    partner = device_at(q ^ 1)
    bulk = [
        pltpu.make_async_remote_copy(
            a, b, far_send.at[i], far_recv.at[i], device_id=partner, device_id_type=MESH
        )
        for i, (a, b) in enumerate(((d, dp), (x, xp), (pts, ptp), (sk, skp), (w_own, wp)))
    ]
    for copy in bulk[:4]:
        copy.start()

    def leaf(l, carry):
        at = pl.ds(pl.multiple_of(l * LEAF, LEAF), LEAF)
        vh, vl = split(jnp.concatenate([d[:, at], x[:, at]], axis=0))
        bh, bl = split(lb[:, at])
        both = dot_nt(jnp.concatenate([bh, bl], axis=0), vh)
        w_own[pl.ds(pl.multiple_of(l * RANK, RANK), RANK), :] = (
            both[:RANK] + both[RANK:] + dot_nt(bh, vl)
        )
        return carry

    lax.fori_loop(0, LEAVES, leaf, 0, unroll=4)
    bulk[4].start()
    buf[0, 0] = dot3(db[...], w_own[...])
    core = exchange(buf, 0, CORE, send, recv)
    for copy in core:
        copy.start()
    row = lax.broadcasted_iota(jnp.int32, (128, 128), 0)
    col = lax.broadcasted_iota(jnp.int32, (128, 128), 1)
    for c in range(1, 7):
        start = 64 * (128 - 2 * (128 >> c)) + 128 * lax.shift_right_logical(q, c + 1)
        source, target = features(nc[:, pl.ds(pl.multiple_of(start, 128), 128)])
        full = kern(dot(source.T.astype(bf16), target.astype(bf16)))
        kmask[c - 1] = jnp.where((row < 64) == (col < 64), 0.0, full)
    for load in loads:
        load.wait()

    def own_pair(number, a):
        e = a & 2
        return jnp.concatenate([buf[number, a ^ e], buf[number, a ^ (e + 1)]], axis=0)

    def pair(number, a, b):
        return jnp.concatenate([buf[number, a ^ (2 * b)], buf[number, a ^ (2 * b + 1)]], axis=0)

    stacks = [None] * 7
    for copy in core:
        copy.wait()
    h = q & 1
    bottom = jnp.concatenate([buf[0, h], buf[0, h ^ 1]], axis=0)
    current = dot3(mats[0], bottom)
    for r in range(3):
        buf[r + 1, 0] = current
        copies = exchange(buf, r + 1, RINGS[r], send, recv)
        for copy in copies:
            copy.start()
        for copy in copies:
            copy.wait()
        a = lax.shift_right_logical(q, 2 * r + 1) & 3
        stacks[2 * r + 1] = own_pair(r + 1, a)
        stacks[2 * r + 2] = jnp.concatenate(
            [dot3(mats[3 * r + 1 + b], pair(r + 1, a, b)) for b in range(2)], axis=0
        )
        if r < 2:
            current = dot3(mats[3 * r + 3], stacks[2 * r + 2])

    def half(value, c):
        return jnp.where((lax.shift_right_logical(q, c) & 1) == 0, value[:64], value[64:])

    down = half(dot3(kmask[5], stacks[6]), 6)
    for c in range(6, 0, -1):
        if c % 2:
            matrix = mats[(c - 1) // 2 * 3]
        else:
            matrix = mats[(c - 2) // 2 * 3 + 1 + (lax.shift_right_logical(q, c) & 1)]
        children = dot3(matrix.T, down)
        if c > 1:
            children = children + dot3(kmask[c - 2], stacks[c - 1])
        down = half(children, c - 1)
    z0[...] = down
    for copy in bulk:
        copy.wait()


def apply_kernel(
    count, tg, sr, far, d, x, dp, xp, pts, ptp, sk, skp, w_own, wp, lb, db, z0, res,
    hd, hx, sums,
    vt, fs, ft, wt, fte, fto, fsk, zl, acc, kh, kl,
):
    def leaf_tables(l, carry):
        at = pl.ds(pl.multiple_of(l * LEAF, LEAF), LEAF)
        for side, (dd, xx, pp) in enumerate(((d, x, pts), (dp, xp, ptp))):
            hi, lo = split(jnp.concatenate([dd[:, at], xx[:, at]], axis=0))
            vt[side * LEAVES + l] = jnp.concatenate([hi, lo], axis=0)
            source, target = features(pp[:, at])
            fs[side * LEAVES + l] = source.T.astype(bf16)
            if side == 0:
                ft[l] = target.astype(bf16)
        acc[l] = jnp.zeros((2 * COLS, LEAF), f32)
        return carry

    lax.fori_loop(0, LEAVES, leaf_tables, 0, unroll=2)
    vt[2 * LEAVES] = jnp.zeros((4 * COLS, LEAF), bf16)
    fs[2 * LEAVES] = jnp.zeros((LEAF, 64), bf16)
    wt[2 * LEAVES] = jnp.zeros((RANK, 4 * COLS), bf16)
    fte[2 * LEAVES] = jnp.zeros((64, 128), bf16)
    fto[2 * LEAVES] = jnp.zeros((64, 128), bf16)

    def skel_tables(m, carry):
        at = pl.ds(pl.multiple_of(m * 128, 128), 128)
        low = lax.broadcasted_iota(jnp.int32, (64, 128), 1) < 64
        for side, (ss, ww) in enumerate(((sk, w_own), (skp, wp))):
            source, target = features(ss[:, at])
            turned = pltpu.roll(target, 64, 1)
            one = side * LEAVES + 2 * m
            fte[one] = jnp.where(low, target, 0.0).astype(bf16)
            fto[one] = jnp.where(low, 0.0, turned).astype(bf16)
            fte[one + 1] = jnp.where(low, turned, 0.0).astype(bf16)
            fto[one + 1] = jnp.where(low, 0.0, target).astype(bf16)
            for i in range(2):
                hi, lo = split(ww[pl.ds(pl.multiple_of(m * 128 + i * 64, 64), 64), :])
                wt[one + i] = jnp.concatenate([hi, lo], axis=1)
            if side == 0:
                flipped = source.T.astype(bf16)
                fsk[2 * m] = flipped[:64]
                fsk[2 * m + 1] = flipped[64:]
        dh, dl = split(db[:, at].T)
        zh, zlo = split(z0[...])
        part = dot(dh, zh) + (dot(dh, zlo) + dot(dl, zh))
        zl[2 * m] = part[:64]
        zl[2 * m + 1] = part[64:]
        return carry

    lax.fori_loop(0, LEAVES // 2, skel_tables, 0, unroll=2)

    def tile(k, b):
        hi, lo = split(kern(dot(fs[sr[k]], ft[tg[k]])))
        kh[b] = hi
        kl[b] = lo

    def multiply(k, b):
        v = vt[sr[k]]
        both = dot(v, kh[b])
        acc[tg[k]] += both[: 2 * COLS] + both[2 * COLS :] + dot(v[: 2 * COLS], kl[b])

    for j in range(AHEAD):
        tile(j, j)

    def near(i, carry):
        for j in range(BUFS):
            k = i * BUFS + j
            multiply(k, j)
            tile(jnp.minimum(k + AHEAD, SLOTS - 1), (j + AHEAD) % BUFS)
        return carry

    lax.fori_loop(0, lax.div(count[0] + (BUFS - 1), BUFS), near, 0)

    def finish(l, carry):
        lanes = []
        rows = []
        for j in range(4):
            one, two = far[l * 8 + 2 * j], far[l * 8 + 2 * j + 1]
            lanes.append(fte[one] + fto[two])
            rows += [wt[one], wt[two]]
        kk = kern(dot(fsk[l], jnp.concatenate(lanes, axis=1)))
        hi, lo = split(kk)
        got = dot(jnp.concatenate([hi, lo], axis=0), jnp.concatenate(rows, axis=0))
        z = zl[l] + got[:64, :128] + got[:64, 128:] + got[64:, :128]
        zh = z.astype(bf16).astype(f32)
        zcat = jnp.concatenate([zh, z - zh, zh], axis=0).T.astype(bf16)
        at = pl.ds(pl.multiple_of(l * LEAF, LEAF), LEAF)
        bh, bl = split(lb[:, at])
        out = acc[l] + dot(zcat, jnp.concatenate([bh, bh, bl], axis=0))
        dl = d[:, at]
        image = noise_level * dl + out[:COLS]
        hd[:, at] = image
        hx[:, at] = noise_level * x[:, at] + out[COLS:]
        r = res[:, at]

        def fold(value):
            return value[:, :128] + value[:, 128:]

        curv, cross, square, old = carry
        return (
            curv + fold(dl * image),
            cross + fold(r * image),
            square + fold(image * image),
            old + fold(r * r),
        )

    zero = jnp.zeros((COLS, 128), f32)
    totals = lax.fori_loop(0, LEAVES, finish, (zero,) * 4, unroll=2)
    lane = lax.broadcasted_iota(jnp.int32, (COLS, 128), 1)
    packed = zero
    for i, total in enumerate(totals):
        packed = jnp.where(lane == i, jnp.sum(total, axis=1, keepdims=True), packed)
    packed = jnp.concatenate([packed, zero], axis=0)
    sums[...] = packed.T[:8]


def reduce_kernel(part, out, buf, send, recv):
    every = CORE + sum(RINGS, ())
    greet(every)
    value = part[...]
    await_greetings(every)
    for r, masks in enumerate((CORE,) + RINGS):
        buf[r, 0] = value
        copies = exchange(buf, r, masks, send, recv)
        for copy in copies:
            copy.start()
        for copy in copies:
            copy.wait()
        value = buf[r, 0] + buf[r, 1]
        if len(masks) == 3:
            value = value + (buf[r, 2] + buf[r, 3])
    curv, cross, square, old = value[0:1], value[1:2], value[2:3], value[3:4]
    alpha = old / curv
    new = old - 2.0 * alpha * cross + alpha * alpha * square
    beta = new / old
    row = lax.broadcasted_iota(jnp.int32, (8, 128), 0)
    out[...] = jnp.where(row == 0, alpha, jnp.where(row == 1, beta, 0.0))


def pair_lists(near_list):
    flat = near_list.reshape(-1)
    number = flat.shape[0]
    live = flat >= 0
    idx = jnp.arange(number, dtype=jnp.int32)
    place = jnp.sum(jnp.where(idx[:, None] > idx[None, :], live[None, :], False).astype(jnp.int32), axis=1)
    slot = jnp.arange(SLOTS, dtype=jnp.int32)
    hit = (place[None, :] == slot[:, None]) & live[None, :]
    code = jnp.sum(jnp.where(hit, (idx // 8)[None, :] * 128 + flat[None, :] - (31 * 128 + 64), 0), axis=1)
    code = code + (31 * 128 + 64)
    total = jnp.sum(live.astype(jnp.int32))
    return total[None], code // 128, code % 128


def shards(
    rhs, iterate, residual, direction, points, skeletons, leaf_basis, device_basis, transfer,
    node_coords, near_list, far_list,
):
    vm = pl.BlockSpec(memory_space=pltpu.VMEM)
    sm = pl.BlockSpec(memory_space=pltpu.SMEM)
    hbm = pl.BlockSpec(memory_space=pl.ANY)
    count, tg, sr = pair_lists(near_list)
    far = jnp.where(far_list < 0, 64, far_list).reshape(-1)
    wide = jax.ShapeDtypeStruct((COLS, LEAVES * LEAF), f32)
    weights = jax.ShapeDtypeStruct((LEAVES * RANK, 2 * COLS), f32)
    z0, w_own, dp, xp, wp, ptp, skp = pl.pallas_call(
        climb_kernel,
        out_shape=(
            jax.ShapeDtypeStruct((RANK, 2 * COLS), f32),
            weights,
            wide,
            wide,
            weights,
            jax.ShapeDtypeStruct(points.shape, f32),
            jax.ShapeDtypeStruct(skeletons.shape, f32),
        ),
        in_specs=[vm, vm, vm, vm, hbm, vm, vm, vm],
        out_specs=(vm,) * 7,
        scratch_shapes=[
            pltpu.VMEM((9, 64, 128), f32),
            pltpu.VMEM((6, 128, 128), f32),
            pltpu.VMEM((4, 4, 64, 128), f32),
            pltpu.SemaphoreType.DMA((6,)),
            pltpu.SemaphoreType.DMA((5,)),
            pltpu.SemaphoreType.DMA((5,)),
            pltpu.SemaphoreType.DMA((4, 3)),
            pltpu.SemaphoreType.DMA((4, 3)),
        ],
        compiler_params=pltpu.CompilerParams(
            collective_id=0, has_side_effects=True, vmem_limit_bytes=40 << 20
        ),
    )(direction, iterate, leaf_basis, device_basis, transfer, node_coords, points, skeletons)
    hd, hx, sums = pl.pallas_call(
        apply_kernel,
        out_shape=(wide, wide, jax.ShapeDtypeStruct((8, 128), f32)),
        in_specs=[sm] * 4 + [vm] * 14,
        out_specs=(vm,) * 3,
        scratch_shapes=[
            pltpu.VMEM((65, 256, 256), bf16),
            pltpu.VMEM((65, 256, 64), bf16),
            pltpu.VMEM((32, 64, 256), bf16),
            pltpu.VMEM((65, 64, 256), bf16),
            pltpu.VMEM((65, 64, 128), bf16),
            pltpu.VMEM((65, 64, 128), bf16),
            pltpu.VMEM((32, 64, 64), bf16),
            pltpu.VMEM((32, 64, 128), f32),
            pltpu.VMEM((32, 128, 256), f32),
            pltpu.VMEM((BUFS, 256, 256), bf16),
            pltpu.VMEM((BUFS, 256, 256), bf16),
        ],
        compiler_params=pltpu.CompilerParams(vmem_limit_bytes=60 << 20),
    )(
        count, tg, sr, far, direction, iterate, dp, xp, points, ptp, skeletons, skp, w_own, wp,
        leaf_basis, device_basis, z0, residual,
    )
    scalars = pl.pallas_call(
        reduce_kernel,
        out_shape=jax.ShapeDtypeStruct((8, 128), f32),
        in_specs=[vm],
        out_specs=vm,
        scratch_shapes=[
            pltpu.VMEM((4, 4, 8, 128), f32),
            pltpu.SemaphoreType.DMA((4, 3)),
            pltpu.SemaphoreType.DMA((4, 3)),
        ],
        compiler_params=pltpu.CompilerParams(collective_id=1, has_side_effects=True),
    )(sums)
    alpha = scalars[0, :COLS][:, None]
    beta = scalars[1, :COLS][:, None]
    new_iterate = iterate + alpha * direction
    new_residual = residual - alpha * hd
    new_direction = new_residual + beta * direction
    true_residual = rhs - (hx + alpha * hd)
    return (new_iterate, new_residual, new_direction, true_residual)


def solution(mesh):
    wide = P(None, ("leaf", "sub"))
    rows = P(("leaf", "sub"), None)
    return jax.shard_map(
        shards,
        mesh=mesh,
        in_specs=(wide,) * 8 + (P(), P(), rows, rows),
        out_specs=(wide,) * 4,
        check_vma=False,
    )
```

```python
import functools
import math

import jax
import jax.numpy as jnp
from jax import lax
from jax.experimental import pallas as pl
from jax.experimental.pallas import tpu as pltpu
from jax.sharding import PartitionSpec as P

MESH = pl.DeviceIdType.MESH
f32, bf16 = jnp.float32, jnp.bfloat16
noise_level = 1.0
amplitude = 0.1
length_scale = 1.0
LN2 = math.log(2.0)
COORD = math.sqrt(3.0) / length_scale / LN2
LEAVES, LEAF, RANK, COLS = 32, 256, 64, 64
SLOTS, BUFS, AHEAD = 200, 8, 4
ENDS, FARS = SLOTS, SLOTS + LEAVES
STEPS, CHUNKS = 24, 4
RING_AT, DOWN_AT = (3, 7, 11), 15
VMEM_LIMIT = 63 << 20
CORE = (1,)
RINGS = ((2, 4, 6), (8, 16, 24), (32, 64, 96))


def dot(a, b):
    return lax.dot_general(a, b, (((1,), (0,)), ((), ())), preferred_element_type=f32)


def dot_nt(a, b):
    return lax.dot_general(a, b, (((1,), (1,)), ((), ())), preferred_element_type=f32)


def split(a):
    hi = a.astype(bf16)
    return hi, (a - hi.astype(f32)).astype(bf16)


def dot3(a, b):
    ah, al = split(a)
    bh, bl = split(b)
    return dot(ah, bh) + (dot(ah, bl) + dot(al, bh))


def kern(u):
    t = jnp.maximum(u, 1e-12)
    s = t * lax.rsqrt(t)
    return (amplitude + (amplitude * LN2) * s) * jnp.exp2(-s)


def pieces(a):
    one = a.astype(bf16).astype(f32)
    rest = a - one
    two = rest.astype(bf16).astype(f32)
    three = (rest - two).astype(bf16).astype(f32)
    return one, two, three


def features(coords):
    a = coords * COORD
    a1, a2, a3 = pieces(a)
    n1, n2, n3 = pieces(jnp.sum(a * a, axis=0, keepdims=True))
    row = lax.broadcasted_iota(jnp.int32, a.shape, 0)
    norm = jnp.where((row == 0) | (row == 3), n1, jnp.where((row == 1) | (row == 4), n2, n3))
    zero = jnp.zeros_like(a)
    src_norm = jnp.where(row < 3, norm, jnp.where(row < 6, 1.0, 0.0))
    tgt_norm = jnp.where(row < 3, 1.0, jnp.where(row < 6, norm, 0.0))
    s1, s2, s3 = -2.0 * a1, -2.0 * a2, -2.0 * a3
    source = jnp.concatenate([s1, s1, s2, s2, s1, s3, src_norm, zero], axis=0)
    target = jnp.concatenate([a1, a2, a1, a2, a3, a1, tgt_norm, zero], axis=0)
    return source, target


def tree_position():
    return lax.axis_index("sub") * 32 + lax.axis_index("leaf")


def device_at(q):
    return (lax.rem(q, 32), lax.div(q, 32))


def greet(masks):
    q = tree_position()
    barrier = pltpu.get_barrier_semaphore()
    for mask in masks:
        pl.semaphore_signal(barrier, inc=1, device_id=device_at(q ^ mask), device_id_type=MESH)


def await_greetings(masks):
    pl.semaphore_wait(pltpu.get_barrier_semaphore(), len(masks))


def exchange(buf, number, masks, send, recv):
    q = tree_position()
    return [
        pltpu.make_async_remote_copy(
            buf.at[number, 0],
            buf.at[number, i + 1],
            send.at[number, i],
            recv.at[number, i],
            device_id=device_at(q ^ mask),
            device_id_type=MESH,
        )
        for i, mask in enumerate(masks)
    ]


def step_kernel(
    meta, d_in, x_in, lb_in, db_in, transfer, nc_in, pts_in, sk_in, res_in,
    hd_out, hx_out, scalars,
    d, x, lb, db, nc, pts, sk, dp, xp, ptp, skp, w_own, wp,
    mats, kmask, buf, stk, z0, vt, fs, ft, wt, fte, fto, fsk, zl, zt, terms, kh, kl, tot, abuf,
    in_sem, mat_sem, far_send, far_recv, send, recv, asend, arecv, out_sem,
):
    q = tree_position()
    every = CORE + sum(RINGS, ())
    greet(every)
    chunk = LEAVES * LEAF // CHUNKS
    loads = [
        pltpu.make_async_copy(a, b, in_sem.at[i])
        for i, (a, b) in enumerate(((pts_in, pts), (sk_in, sk), (nc_in, nc), (db_in, db)))
    ]
    for load in loads[:1]:
        load.start()
    parts = []
    for c in range(CHUNKS):
        at = pl.ds(c * chunk, chunk)
        parts.append([
            pltpu.make_async_copy(a.at[:, at], b.at[:, at], in_sem.at[5 + 3 * c + i])
            for i, (a, b) in enumerate(((d_in, d), (x_in, x), (lb_in, lb)))
        ])
        for load in parts[-1]:
            load.start()
        if c == 0:
            for load in loads[1:]:
                load.start()
    spots = []
    for c in range(1, 7):
        base = 128 - 2 * (128 >> c)
        node = lax.shift_right_logical(q, c)
        if c % 2:
            spots.append((base + node, 1, (c - 1) // 2 * 3))
        else:
            spots.append((base + (node & -2), 2, (c - 2) // 2 * 3 + 1))
    mat_loads = [
        pltpu.make_async_copy(transfer.at[pl.ds(at, n)], mats.at[pl.ds(slot, n)], mat_sem.at[i])
        for i, (at, n, slot) in enumerate(spots)
    ]
    for load in mat_loads:
        load.start()

    def lanes(l, width):
        return pl.ds(pl.multiple_of(l * width, width), width)

    loads[0].wait()

    def own_points(l, carry):
        source, target = features(pts[:, lanes(l, LEAF)])
        fs[l] = source.T.astype(bf16)
        ft[l] = target.astype(bf16)
        return carry

    lax.fori_loop(0, LEAVES, own_points, 0, unroll=4)
    await_greetings(every)
    partner = device_at(q ^ 1)
    bulk = [
        pltpu.make_async_remote_copy(
            a, b, far_send.at[i], far_recv.at[i], device_id=partner, device_id_type=MESH
        )
        for i, (a, b) in enumerate(
            ((pts_in, ptp), (d_in, dp), (x_in, xp), (sk_in, skp), (w_own, wp))
        )
    ]
    for copy in bulk[:4]:
        copy.start()

    def leaf(l, carry):
        at = lanes(l, LEAF)
        vh, vl = split(jnp.concatenate([d[:, at], x[:, at]], axis=0))
        vt[l] = jnp.concatenate([vh, vl], axis=0)
        bh, bl = split(lb[:, at])
        both = dot_nt(jnp.concatenate([bh, bl], axis=0), vh)
        w_own[lanes(l, RANK), :] = both[:RANK] + both[RANK:] + dot_nt(bh, vl)
        return carry

    for c in range(CHUNKS):
        for load in parts[c]:
            load.wait()
        lax.fori_loop(c * LEAVES // CHUNKS, (c + 1) * LEAVES // CHUNKS, leaf, 0, unroll=4)
    bulk[4].start()
    for load in loads[1:]:
        load.wait()
    buf[0, 0] = dot3(db[...], w_own[...])
    for copy in exchange(buf, 0, CORE, send, recv):
        copy.start()

    row = lax.broadcasted_iota(jnp.int32, (128, 128), 0)
    col = lax.broadcasted_iota(jnp.int32, (128, 128), 1)
    for c in range(1, 7):
        start = 64 * (128 - 2 * (128 >> c)) + 128 * lax.shift_right_logical(q, c + 1)
        source, target = features(nc[:, pl.ds(pl.multiple_of(start, 128), 128)])
        full = kern(dot(source.T.astype(bf16), target.astype(bf16)))
        kmask[c - 1] = jnp.where((row < 64) == (col < 64), 0.0, full)
    for load in mat_loads:
        load.wait()

    def skel_tables(side, ss, ww):
        low = lax.broadcasted_iota(jnp.int32, (64, 128), 1) < 64

        def one_pair(m, carry):
            source, target = features(ss[:, lanes(m, 128)])
            turned = pltpu.roll(target, 64, 1)
            one = side * LEAVES + 2 * m
            fte[one] = jnp.where(low, target, 0.0).astype(bf16)
            fto[one] = jnp.where(low, 0.0, turned).astype(bf16)
            fte[one + 1] = jnp.where(low, turned, 0.0).astype(bf16)
            fto[one + 1] = jnp.where(low, 0.0, target).astype(bf16)
            for i in range(2):
                hi, lo = split(ww[pl.ds(pl.multiple_of(m * 128 + i * 64, 64), 64), :])
                wt[one + i] = jnp.concatenate([hi, lo], axis=1)
            if side == 0:
                flipped = source.T.astype(bf16)
                fsk[2 * m] = flipped[:64]
                fsk[2 * m + 1] = flipped[64:]
            return carry

        lax.fori_loop(0, LEAVES // 2, one_pair, 0, unroll=4)

    skel_tables(0, sk, w_own)
    vt[2 * LEAVES] = jnp.zeros((4 * COLS, LEAF), bf16)
    fs[2 * LEAVES] = jnp.zeros((LEAF, 64), bf16)
    wt[2 * LEAVES] = jnp.zeros((RANK, 4 * COLS), bf16)
    fte[2 * LEAVES] = jnp.zeros((64, 128), bf16)
    fto[2 * LEAVES] = jnp.zeros((64, 128), bf16)
    terms[0] = jnp.zeros((2 * COLS, LEAF), f32)
    zero = jnp.zeros((COLS, 128), f32)
    for i in range(4):
        tot[i] = zero

    def pair(number, a, b):
        return jnp.concatenate([buf[number, a ^ (2 * b)], buf[number, a ^ (2 * b + 1)]], axis=0)

    def half(value, c):
        return jnp.where((lax.shift_right_logical(q, c) & 1) == 0, value[:64], value[64:])

    def climb_core():
        for copy in exchange(buf, 0, CORE, send, recv):
            copy.wait()
        h = q & 1
        bottom = jnp.concatenate([buf[0, h], buf[0, h ^ 1]], axis=0)
        buf[1, 0] = dot3(mats[0], bottom)
        for copy in exchange(buf, 1, RINGS[0], send, recv):
            copy.start()

    def climb_ring(r):
        for copy in exchange(buf, r + 1, RINGS[r], send, recv):
            copy.wait()
        a = lax.shift_right_logical(q, 2 * r + 1) & 3
        e = a & 2
        stk[2 * r] = jnp.concatenate([buf[r + 1, a ^ e], buf[r + 1, a ^ (e + 1)]], axis=0)
        upper = jnp.concatenate(
            [dot3(mats[3 * r + 1 + b], pair(r + 1, a, b)) for b in range(2)], axis=0
        )
        stk[2 * r + 1] = upper
        if r < 2:
            buf[r + 2, 0] = dot3(mats[3 * r + 3], upper)
            for copy in exchange(buf, r + 2, RINGS[r + 1], send, recv):
                copy.start()

    def descend():
        down = half(dot3(kmask[5], stk[5]), 6)
        for c in range(6, 0, -1):
            if c % 2:
                matrix = mats[(c - 1) // 2 * 3]
            else:
                matrix = mats[(c - 2) // 2 * 3 + 1 + (lax.shift_right_logical(q, c) & 1)]
            children = dot3(matrix.T, down)
            if c > 1:
                children = children + dot3(kmask[c - 2], stk[c - 2])
            down = half(children, c - 1)
        z0[...] = down

    climb_core()

    for copy in bulk[:3]:
        copy.wait()

    def partner_points(l, carry):
        at = lanes(l, LEAF)
        source, target = features(ptp[:, at])
        fs[LEAVES + l] = source.T.astype(bf16)
        hi, lo = split(jnp.concatenate([dp[:, at], xp[:, at]], axis=0))
        vt[LEAVES + l] = jnp.concatenate([hi, lo], axis=0)
        return carry

    lax.fori_loop(0, LEAVES, partner_points, 0, unroll=4)
    res_load = pltpu.make_async_copy(res_in, dp, in_sem.at[4])
    res_load.start()

    def tile(k, b):
        code = meta[k]
        hi, lo = split(kern(dot(fs[code & 127], ft[lax.shift_right_logical(code, 7) & 31])))
        kh[b] = hi
        kl[b] = lo

    def multiply(k, b):
        code = meta[k]
        v = vt[code & 127]
        keep = lax.shift_right_logical(code, 12).astype(f32)
        both = dot(v, kh[b])
        terms[k + 1] = terms[k] * keep + (
            both[: 2 * COLS] + both[2 * COLS :] + dot(v[: 2 * COLS], kl[b])
        )

    for j in range(AHEAD):
        tile(j, j)

    def near(i, carry):
        for r in range(3):
            @pl.when(i == RING_AT[r])
            def _():
                climb_ring(r)

        @pl.when(i == DOWN_AT)
        def _():
            descend()

        for j in range(BUFS):
            k = i * BUFS + j
            multiply(k, j)
            tile(k + AHEAD, (j + AHEAD) % BUFS)
        return carry

    lax.fori_loop(0, STEPS, near, 0)

    for copy in bulk[3:]:
        copy.wait()
    skel_tables(1, skp, wp)

    def down_to_leaves(m, carry):
        dh, dl = split(db[:, lanes(m, 128)].T)
        zh, zlo = split(z0[...])
        part = dot(dh, zh) + (dot(dh, zlo) + dot(dl, zh))
        zl[2 * m] = part[:64]
        zl[2 * m + 1] = part[64:]
        return carry

    lax.fori_loop(0, LEAVES // 2, down_to_leaves, 0, unroll=4)

    def farther(l, carry):
        across = []
        rows = []
        for j in range(4):
            one, two = meta[FARS + l * 8 + 2 * j], meta[FARS + l * 8 + 2 * j + 1]
            across.append(fte[one] + fto[two])
            rows += [wt[one], wt[two]]
        hi, lo = split(kern(dot(fsk[l], jnp.concatenate(across, axis=1))))
        got = dot(jnp.concatenate([hi, lo], axis=0), jnp.concatenate(rows, axis=0))
        zl[l] += got[:64, :128] + got[:64, 128:] + got[64:, :128]
        return carry

    lax.fori_loop(0, LEAVES, farther, 0, unroll=4)

    def turn(l, carry):
        z = zl[l]
        zh = z.astype(bf16).astype(f32)
        zt[l] = jnp.concatenate([zh, z - zh], axis=0).T.astype(bf16)
        return carry

    lax.fori_loop(0, LEAVES, turn, 0, unroll=8)
    res_load.wait()

    def fold(value):
        return value[:, :128] + value[:, 128:]

    def finish(l, carry):
        at = lanes(l, LEAF)
        bh, bl = split(lb[:, at])
        zz = zt[l]
        out = terms[meta[ENDS + l]] + (
            dot(zz, jnp.concatenate([bh, bh], axis=0)) + dot(zz[:, :64], bl)
        )
        dl = d[:, at]
        r = dp[:, at]
        image = noise_level * dl + out[:COLS]
        tot[0] += fold(dl * image)
        tot[1] += fold(r * image)
        tot[2] += fold(image * image)
        tot[3] += fold(r * r)
        d[:, at] = image
        x[:, at] = noise_level * x[:, at] + out[COLS:]
        return carry

    lax.fori_loop(0, LEAVES, finish, 0, unroll=4)
    outs = [
        pltpu.make_async_copy(a, b, out_sem.at[i])
        for i, (a, b) in enumerate(((d, hd_out), (x, hx_out)))
    ]
    for out in outs:
        out.start()

    lane = lax.broadcasted_iota(jnp.int32, (COLS, 128), 1)
    packed = zero
    for i in range(4):
        packed = jnp.where(lane == i, jnp.sum(tot[i], axis=1, keepdims=True), packed)
    value = jnp.concatenate([packed, zero], axis=0).T[:8]
    for r, masks in enumerate((CORE,) + RINGS):
        abuf[r, 0] = value
        copies = exchange(abuf, r, masks, asend, arecv)
        for copy in copies:
            copy.start()
        for copy in copies:
            copy.wait()
        value = abuf[r, 0] + abuf[r, 1]
        if len(masks) == 3:
            value = value + (abuf[r, 2] + abuf[r, 3])
    curv, cross, square, old = value[0:1], value[1:2], value[2:3], value[3:4]
    alpha = old / curv
    new = old - 2.0 * alpha * cross + alpha * alpha * square
    beta = new / old
    eight = lax.broadcasted_iota(jnp.int32, (8, 128), 0)
    scalars[...] = jnp.where(eight == 0, alpha, jnp.where(eight == 1, beta, 0.0))
    for out in outs:
        out.wait()


def lists(near_list, far_list):
    counts = jnp.sum((near_list >= 0).astype(jnp.int32), axis=1)
    leaf = jnp.arange(LEAVES, dtype=jnp.int32)
    before = jnp.sum(jnp.where(leaf[:, None] > leaf[None, :], counts[None, :], 0), axis=1)
    place = before[:, None] + jnp.arange(8, dtype=jnp.int32)[None, :]
    first = jnp.arange(8, dtype=jnp.int32)[None, :] == 0
    code = near_list + leaf[:, None] * 128 + jnp.where(first, 0, 4096)
    nothing = 64 + 31 * 128 + 4096
    slot = jnp.arange(SLOTS, dtype=jnp.int32)[:, None, None]
    hit = (place[None] == slot) & (near_list >= 0)[None]
    pairs = jnp.sum(jnp.where(hit, code[None] - nothing, 0), axis=(1, 2)) + nothing
    far = jnp.where(far_list < 0, 64, far_list).reshape(-1)
    return jnp.concatenate([pairs, before + counts, far])


def shards(
    rhs, iterate, residual, direction, points, skeletons, leaf_basis, device_basis, transfer,
    node_coords, near_list, far_list,
):
    vm = pl.BlockSpec(memory_space=pltpu.VMEM)
    sm = pl.BlockSpec(memory_space=pltpu.SMEM)
    hbm = pl.BlockSpec(memory_space=pl.ANY)
    wide = jax.ShapeDtypeStruct((COLS, LEAVES * LEAF), f32)
    big = pltpu.VMEM((COLS, LEAVES * LEAF), f32)
    weights = pltpu.VMEM((LEAVES * RANK, 2 * COLS), f32)
    point_buf = pltpu.VMEM(points.shape, f32)
    skel_buf = pltpu.VMEM(skeletons.shape, f32)
    dma = pltpu.SemaphoreType.DMA
    hd, hx, scalars = pl.pallas_call(
        step_kernel,
        out_shape=(wide, wide, jax.ShapeDtypeStruct((8, 128), f32)),
        in_specs=[sm] + [hbm] * 9,
        out_specs=(hbm, hbm, vm),
        scratch_shapes=[
            big, big, big,
            pltpu.VMEM(device_basis.shape, f32),
            pltpu.VMEM(node_coords.shape, f32),
            point_buf, skel_buf,
            big, big, point_buf, skel_buf, weights, weights,
            pltpu.VMEM((9, 64, 128), f32),
            pltpu.VMEM((6, 128, 128), f32),
            pltpu.VMEM((4, 4, 64, 128), f32),
            pltpu.VMEM((6, 128, 128), f32),
            pltpu.VMEM((64, 128), f32),
            pltpu.VMEM((65, 256, 256), bf16),
            pltpu.VMEM((65, 256, 64), bf16),
            pltpu.VMEM((32, 64, 256), bf16),
            pltpu.VMEM((65, 64, 256), bf16),
            pltpu.VMEM((65, 64, 128), bf16),
            pltpu.VMEM((65, 64, 128), bf16),
            pltpu.VMEM((32, 64, 64), bf16),
            pltpu.VMEM((32, 64, 128), f32),
            pltpu.VMEM((32, 128, 128), bf16),
            pltpu.VMEM((STEPS * BUFS + 1, 128, 256), f32),
            pltpu.VMEM((BUFS, 256, 256), bf16),
            pltpu.VMEM((BUFS, 256, 256), bf16),
            pltpu.VMEM((4, 64, 128), f32),
            pltpu.VMEM((4, 4, 8, 128), f32),
            dma((5 + 3 * CHUNKS,)), dma((6,)), dma((5,)), dma((5,)),
            dma((4, 3)), dma((4, 3)), dma((4, 3)), dma((4, 3)), dma((2,)),
        ],
        compiler_params=pltpu.CompilerParams(
            collective_id=0, has_side_effects=True, vmem_limit_bytes=VMEM_LIMIT
        ),
    )(
        lists(near_list, far_list), direction, iterate, leaf_basis, device_basis, transfer,
        node_coords, points, skeletons, residual,
    )
    alpha = scalars[0, :COLS][:, None]
    beta = scalars[1, :COLS][:, None]
    new_iterate = iterate + alpha * direction
    new_residual = residual - alpha * hd
    new_direction = new_residual + beta * direction
    true_residual = rhs - (hx + alpha * hd)
    return (new_iterate, new_residual, new_direction, true_residual)


def solution(mesh):
    wide = P(None, ("leaf", "sub"))
    rows = P(("leaf", "sub"), None)
    return jax.shard_map(
        shards,
        mesh=mesh,
        in_specs=(wide,) * 8 + (P(), P(), rows, rows),
        out_specs=(wide,) * 4,
        check_vma=False,
    )
```

```python
import functools
import math

import jax
import jax.numpy as jnp
from jax import lax
from jax.experimental import pallas as pl
from jax.experimental.pallas import tpu as pltpu
from jax.sharding import PartitionSpec as P

MESH = pl.DeviceIdType.MESH
f32, bf16 = jnp.float32, jnp.bfloat16
noise_level = 1.0
amplitude = 0.1
length_scale = 1.0
LN2 = math.log(2.0)
COORD = math.sqrt(3.0) / length_scale / LN2
LEAVES, LEAF, RANK, COLS = 32, 256, 64, 64
SLOTS, BUFS, AHEAD = 200, 8, 4
ENDS, FARS = SLOTS, SLOTS + LEAVES
STEPS, CHUNKS = 24, 4
RING_AT, DOWN_AT = (5, 9, 13), 17
ALONE, UPDATE = 3, 2048
VMEM_LIMIT = 63 << 20
CORE = (1,)
RINGS = ((2, 4, 6), (8, 16, 24), (32, 64, 96))


def dot(a, b):
    return lax.dot_general(a, b, (((1,), (0,)), ((), ())), preferred_element_type=f32)


def dot_nt(a, b):
    return lax.dot_general(a, b, (((1,), (1,)), ((), ())), preferred_element_type=f32)


def split(a):
    hi = a.astype(bf16)
    return hi, (a - hi.astype(f32)).astype(bf16)


def dot3(a, b):
    ah, al = split(a)
    bh, bl = split(b)
    return dot(ah, bh) + (dot(ah, bl) + dot(al, bh))


def kern(u):
    t = jnp.maximum(u, 1e-12)
    s = t * lax.rsqrt(t)
    return (amplitude + (amplitude * LN2) * s) * jnp.exp2(-s)


def pieces(a):
    one = a.astype(bf16).astype(f32)
    rest = a - one
    two = rest.astype(bf16).astype(f32)
    three = (rest - two).astype(bf16).astype(f32)
    return one, two, three


def features(coords):
    a = coords * COORD
    a1, a2, a3 = pieces(a)
    n1, n2, n3 = pieces(jnp.sum(a * a, axis=0, keepdims=True))
    row = lax.broadcasted_iota(jnp.int32, a.shape, 0)
    norm = jnp.where((row == 0) | (row == 3), n1, jnp.where((row == 1) | (row == 4), n2, n3))
    zero = jnp.zeros_like(a)
    src_norm = jnp.where(row < 3, norm, jnp.where(row < 6, 1.0, 0.0))
    tgt_norm = jnp.where(row < 3, 1.0, jnp.where(row < 6, norm, 0.0))
    s1, s2, s3 = -2.0 * a1, -2.0 * a2, -2.0 * a3
    source = jnp.concatenate([s1, s1, s2, s2, s1, s3, src_norm, zero], axis=0)
    target = jnp.concatenate([a1, a2, a1, a2, a3, a1, tgt_norm, zero], axis=0)
    return source, target


def tree_position():
    return lax.axis_index("sub") * 32 + lax.axis_index("leaf")


def device_at(q):
    return (lax.rem(q, 32), lax.div(q, 32))


def greet(masks):
    q = tree_position()
    barrier = pltpu.get_barrier_semaphore()
    for mask in masks:
        pl.semaphore_signal(barrier, inc=1, device_id=device_at(q ^ mask), device_id_type=MESH)


def await_greetings(masks):
    pl.semaphore_wait(pltpu.get_barrier_semaphore(), len(masks))


def exchange(buf, number, masks, send, recv):
    q = tree_position()
    return [
        pltpu.make_async_remote_copy(
            buf.at[number, 0],
            buf.at[number, i + 1],
            send.at[number, i],
            recv.at[number, i],
            device_id=device_at(q ^ mask),
            device_id_type=MESH,
        )
        for i, mask in enumerate(masks)
    ]


def step_kernel(
    meta, d_in, x_in, lb_in, db_in, transfer, nc_in, pts_in, sk_in, res_in, rhs_in,
    hd_out, gap_out, scalars,
    d, x, lb, db, nc, pts, sk, dp, xp, ptp, skp, w_own, wp,
    mats, kmask, buf, stk, z0, vt, fs, ft, wt, fte, fto, fsk, zl, zt, terms, kh, kl, tot, abuf,
    in_sem, mat_sem, far_send, far_recv, send, recv, asend, arecv, out_sem, late_sem,
):
    q = tree_position()
    every = CORE + sum(RINGS, ())
    greet(every)
    chunk = LEAVES * LEAF // CHUNKS
    loads = [
        pltpu.make_async_copy(a, b, in_sem.at[i])
        for i, (a, b) in enumerate(((pts_in, pts), (sk_in, sk), (nc_in, nc), (db_in, db)))
    ]
    for load in loads[:1]:
        load.start()
    parts = []
    for c in range(CHUNKS):
        at = pl.ds(c * chunk, chunk)
        parts.append([
            pltpu.make_async_copy(a.at[:, at], b.at[:, at], in_sem.at[5 + 3 * c + i])
            for i, (a, b) in enumerate(((d_in, d), (x_in, x), (lb_in, lb)))
        ])
        for load in parts[-1]:
            load.start()
        if c == 0:
            for load in loads[1:]:
                load.start()
    spots = []
    for c in range(1, 7):
        base = 128 - 2 * (128 >> c)
        node = lax.shift_right_logical(q, c)
        if c % 2:
            spots.append((base + node, 1, (c - 1) // 2 * 3))
        else:
            spots.append((base + (node & -2), 2, (c - 2) // 2 * 3 + 1))
    mat_loads = [
        pltpu.make_async_copy(transfer.at[pl.ds(at, n)], mats.at[pl.ds(slot, n)], mat_sem.at[i])
        for i, (at, n, slot) in enumerate(spots)
    ]
    for load in mat_loads:
        load.start()

    def lanes(l, width):
        return pl.ds(pl.multiple_of(l * width, width), width)

    await_greetings(every)
    partner = device_at(q ^ 1)
    bulk = [
        pltpu.make_async_remote_copy(
            a, b, far_send.at[i], far_recv.at[i], device_id=partner, device_id_type=MESH
        )
        for i, (a, b) in enumerate(
            ((pts_in, ptp), (d_in, dp), (x_in, xp), (sk_in, skp), (w_own, wp))
        )
    ]
    for copy in bulk[:4]:
        copy.start()

    loads[0].wait()

    def own_points(l, carry):
        source, target = features(pts[:, lanes(l, LEAF)])
        fs[l] = source.T.astype(bf16)
        ft[l] = target.astype(bf16)
        return carry

    lax.fori_loop(0, LEAVES, own_points, 0, unroll=4)

    def leaf(l, carry):
        at = lanes(l, LEAF)
        vh, vl = split(jnp.concatenate([d[:, at], x[:, at]], axis=0))
        vt[l] = jnp.concatenate([vh, vl], axis=0)
        bh, bl = split(lb[:, at])
        both = dot_nt(jnp.concatenate([bh, bl], axis=0), vh)
        w_own[lanes(l, RANK), :] = both[:RANK] + both[RANK:] + dot_nt(bh, vl)
        return carry

    for c in range(CHUNKS):
        for load in parts[c]:
            load.wait()
        lax.fori_loop(c * LEAVES // CHUNKS, (c + 1) * LEAVES // CHUNKS, leaf, 0, unroll=4)
    bulk[4].start()
    for load in loads[1:]:
        load.wait()
    buf[0, 0] = dot3(db[...], w_own[...])
    for copy in exchange(buf, 0, CORE, send, recv):
        copy.start()

    row = lax.broadcasted_iota(jnp.int32, (128, 128), 0)
    col = lax.broadcasted_iota(jnp.int32, (128, 128), 1)
    for c in range(1, 7):
        start = 64 * (128 - 2 * (128 >> c)) + 128 * lax.shift_right_logical(q, c + 1)
        source, target = features(nc[:, pl.ds(pl.multiple_of(start, 128), 128)])
        full = kern(dot(source.T.astype(bf16), target.astype(bf16)))
        kmask[c - 1] = jnp.where((row < 64) == (col < 64), 0.0, full)
    for load in mat_loads:
        load.wait()

    def skel_tables(side, ss, ww):
        low = lax.broadcasted_iota(jnp.int32, (64, 128), 1) < 64

        def one_pair(m, carry):
            source, target = features(ss[:, lanes(m, 128)])
            turned = pltpu.roll(target, 64, 1)
            one = side * LEAVES + 2 * m
            fte[one] = jnp.where(low, target, 0.0).astype(bf16)
            fto[one] = jnp.where(low, 0.0, turned).astype(bf16)
            fte[one + 1] = jnp.where(low, turned, 0.0).astype(bf16)
            fto[one + 1] = jnp.where(low, 0.0, target).astype(bf16)
            for i in range(2):
                hi, lo = split(ww[pl.ds(pl.multiple_of(m * 128 + i * 64, 64), 64), :])
                wt[one + i] = jnp.concatenate([hi, lo], axis=1)
            if side == 0:
                flipped = source.T.astype(bf16)
                fsk[2 * m] = flipped[:64]
                fsk[2 * m + 1] = flipped[64:]
            return carry

        lax.fori_loop(0, LEAVES // 2, one_pair, 0, unroll=4)

    skel_tables(0, sk, w_own)
    vt[2 * LEAVES] = jnp.zeros((4 * COLS, LEAF), bf16)
    fs[2 * LEAVES] = jnp.zeros((LEAF, 64), bf16)
    wt[2 * LEAVES] = jnp.zeros((RANK, 4 * COLS), bf16)
    fte[2 * LEAVES] = jnp.zeros((64, 128), bf16)
    fto[2 * LEAVES] = jnp.zeros((64, 128), bf16)
    terms[0] = jnp.zeros((2 * COLS, LEAF), f32)
    zero = jnp.zeros((COLS, 128), f32)
    for i in range(4):
        tot[i] = zero

    def pair(number, a, b):
        return jnp.concatenate([buf[number, a ^ (2 * b)], buf[number, a ^ (2 * b + 1)]], axis=0)

    def half(value, c):
        return jnp.where((lax.shift_right_logical(q, c) & 1) == 0, value[:64], value[64:])

    def climb_core():
        for copy in exchange(buf, 0, CORE, send, recv):
            copy.wait()
        h = q & 1
        bottom = jnp.concatenate([buf[0, h], buf[0, h ^ 1]], axis=0)
        buf[1, 0] = dot3(mats[0], bottom)
        for copy in exchange(buf, 1, RINGS[0], send, recv):
            copy.start()

    def climb_ring(r):
        for copy in exchange(buf, r + 1, RINGS[r], send, recv):
            copy.wait()
        a = lax.shift_right_logical(q, 2 * r + 1) & 3
        e = a & 2
        stk[2 * r] = jnp.concatenate([buf[r + 1, a ^ e], buf[r + 1, a ^ (e + 1)]], axis=0)
        upper = jnp.concatenate(
            [dot3(mats[3 * r + 1 + b], pair(r + 1, a, b)) for b in range(2)], axis=0
        )
        stk[2 * r + 1] = upper
        if r < 2:
            buf[r + 2, 0] = dot3(mats[3 * r + 3], upper)
            for copy in exchange(buf, r + 2, RINGS[r + 1], send, recv):
                copy.start()

    def descend():
        down = half(dot3(kmask[5], stk[5]), 6)
        for c in range(6, 0, -1):
            if c % 2:
                matrix = mats[(c - 1) // 2 * 3]
            else:
                matrix = mats[(c - 2) // 2 * 3 + 1 + (lax.shift_right_logical(q, c) & 1)]
            children = dot3(matrix.T, down)
            if c > 1:
                children = children + dot3(kmask[c - 2], stk[c - 2])
            down = half(children, c - 1)
        z0[...] = down

    def tile(k, b):
        code = meta[k]
        hi, lo = split(kern(dot(fs[code & 127], ft[lax.shift_right_logical(code, 7) & 31])))
        kh[b] = hi
        kl[b] = lo

    def multiply(k, b):
        code = meta[k]
        v = vt[code & 127]
        keep = lax.shift_right_logical(code, 12).astype(f32)
        both = dot(v, kh[b])
        terms[k + 1] = terms[k] * keep + (
            both[: 2 * COLS] + both[2 * COLS :] + dot(v[: 2 * COLS], kl[b])
        )

    for j in range(AHEAD):
        tile(j, j)

    def near_step(i):
        for j in range(BUFS):
            k = i * BUFS + j
            multiply(k, j)
            tile(k + AHEAD, (j + AHEAD) % BUFS)

    def near_alone(i, carry):
        near_step(i)
        return carry

    lax.fori_loop(0, ALONE, near_alone, 0)
    climb_core()

    for copy in bulk[:3]:
        copy.wait()

    def partner_points(l, carry):
        at = lanes(l, LEAF)
        source, target = features(ptp[:, at])
        fs[LEAVES + l] = source.T.astype(bf16)
        hi, lo = split(jnp.concatenate([dp[:, at], xp[:, at]], axis=0))
        vt[LEAVES + l] = jnp.concatenate([hi, lo], axis=0)
        return carry

    lax.fori_loop(0, LEAVES, partner_points, 0, unroll=4)
    late = [
        pltpu.make_async_copy(a, b, late_sem.at[i])
        for i, (a, b) in enumerate(((res_in, dp), (rhs_in, xp)))
    ]
    for load in late:
        load.start()

    def near(i, carry):
        for r in range(3):
            @pl.when(i == RING_AT[r])
            def _():
                climb_ring(r)

        @pl.when(i == DOWN_AT)
        def _():
            descend()

        near_step(i)
        return carry

    lax.fori_loop(ALONE, STEPS, near, 0)

    for copy in bulk[3:]:
        copy.wait()
    skel_tables(1, skp, wp)

    def down_to_leaves(m, carry):
        dh, dl = split(db[:, lanes(m, 128)].T)
        zh, zlo = split(z0[...])
        part = dot(dh, zh) + (dot(dh, zlo) + dot(dl, zh))
        zl[2 * m] = part[:64]
        zl[2 * m + 1] = part[64:]
        return carry

    lax.fori_loop(0, LEAVES // 2, down_to_leaves, 0, unroll=4)

    def farther(l, carry):
        across = []
        rows = []
        for j in range(4):
            one, two = meta[FARS + l * 8 + 2 * j], meta[FARS + l * 8 + 2 * j + 1]
            across.append(fte[one] + fto[two])
            rows += [wt[one], wt[two]]
        hi, lo = split(kern(dot(fsk[l], jnp.concatenate(across, axis=1))))
        got = dot(jnp.concatenate([hi, lo], axis=0), jnp.concatenate(rows, axis=0))
        zl[l] += got[:64, :128] + got[:64, 128:] + got[64:, :128]
        return carry

    lax.fori_loop(0, LEAVES, farther, 0, unroll=4)

    def turn(l, carry):
        z = zl[l]
        zh = z.astype(bf16).astype(f32)
        zt[l] = jnp.concatenate([zh, z - zh], axis=0).T.astype(bf16)
        return carry

    lax.fori_loop(0, LEAVES, turn, 0, unroll=8)
    for load in late:
        load.wait()

    def fold(value):
        return value[:, :128] + value[:, 128:]

    def applied(l, at, rows):
        bh, bl = split(lb[:, at])
        zz = zt[l, rows]
        pairs = terms[1 + l, rows] + terms[meta[ENDS + l], rows]
        return pairs + (dot(zz, jnp.concatenate([bh, bh], axis=0)) + dot(zz[:, :64], bl))

    def finish(l, carry):
        at = lanes(l, LEAF)
        dl = d[:, at]
        r = dp[:, at]
        image = noise_level * dl + applied(l, at, pl.ds(0, COLS))
        tot[0] += fold(dl * image)
        tot[1] += fold(r * image)
        tot[2] += fold(image * image)
        tot[3] += fold(r * r)
        d[:, at] = image
        return carry

    def finish_iterate(l, carry):
        at = lanes(l, LEAF)
        x[:, at] = xp[:, at] - (noise_level * x[:, at] + applied(l, at, pl.ds(COLS, COLS)))
        return carry

    lax.fori_loop(0, LEAVES, finish, 0, unroll=4)
    outs = [
        pltpu.make_async_copy(a, b, out_sem.at[i])
        for i, (a, b) in enumerate(((d, hd_out), (x, gap_out)))
    ]
    outs[0].start()

    lane = lax.broadcasted_iota(jnp.int32, (COLS, 128), 1)
    packed = zero
    for i in range(4):
        packed = jnp.where(lane == i, jnp.sum(tot[i], axis=1, keepdims=True), packed)
    value = jnp.concatenate([packed, zero], axis=0).T[:8]
    for r, masks in enumerate((CORE,) + RINGS):
        abuf[r, 0] = value
        copies = exchange(abuf, r, masks, asend, arecv)
        for copy in copies:
            copy.start()
        if r == 1:
            lax.fori_loop(0, LEAVES, finish_iterate, 0, unroll=4)
            outs[1].start()
        for copy in copies:
            copy.wait()
        value = abuf[r, 0] + abuf[r, 1]
        if len(masks) == 3:
            value = value + (abuf[r, 2] + abuf[r, 3])
    curv, cross, square, old = value[0:1], value[1:2], value[2:3], value[3:4]
    alpha = old / curv
    new = old - 2.0 * alpha * cross + alpha * alpha * square
    beta = new / old
    eight = lax.broadcasted_iota(jnp.int32, (8, 128), 0)
    value = jnp.where(eight == 0, alpha, jnp.where(eight == 1, beta, 0.0))
    scalars[...] = jnp.concatenate([value, jnp.zeros((120, 128), f32)], axis=0).T[:COLS]
    for out in outs:
        out.wait()


def lists(near_list, far_list):
    others = jnp.sum((near_list >= 0).astype(jnp.int32), axis=1) - 1
    leaf = jnp.arange(LEAVES, dtype=jnp.int32)
    before = jnp.sum(jnp.where(leaf[:, None] > leaf[None, :], others[None, :], 0), axis=1) + LEAVES
    slot8 = jnp.arange(8, dtype=jnp.int32)[None, :]
    place = jnp.where(slot8 == 0, leaf[:, None], before[:, None] + slot8 - 1)
    code = near_list + leaf[:, None] * 128 + jnp.where(slot8 < 2, 0, 4096)
    nothing = 64 + 31 * 128 + 4096
    slot = jnp.arange(SLOTS, dtype=jnp.int32)[:, None, None]
    hit = (place[None] == slot) & (near_list >= 0)[None]
    pairs = jnp.sum(jnp.where(hit, code[None] - nothing, 0), axis=(1, 2)) + nothing
    ends = jnp.where(others > 0, before + others, 0)
    far = jnp.where(far_list < 0, 64, far_list).reshape(-1)
    return jnp.concatenate([pairs, ends, far])


def update_kernel(scalars, it, d, r, hd, gap, new_it, new_r, new_d, true_r):
    alpha, beta = scalars[:, 0:1], scalars[:, 1:2]
    dd, step = d[...], alpha * hd[...]
    rr = r[...] - step
    new_it[...] = it[...] + alpha * dd
    new_r[...] = rr
    new_d[...] = rr + beta * dd
    true_r[...] = gap[...] - step


def shards(
    rhs, iterate, residual, direction, points, skeletons, leaf_basis, device_basis, transfer,
    node_coords, near_list, far_list,
):
    vm = pl.BlockSpec(memory_space=pltpu.VMEM)
    sm = pl.BlockSpec(memory_space=pltpu.SMEM)
    hbm = pl.BlockSpec(memory_space=pl.ANY)
    wide = jax.ShapeDtypeStruct((COLS, LEAVES * LEAF), f32)
    big = pltpu.VMEM((COLS, LEAVES * LEAF), f32)
    weights = pltpu.VMEM((LEAVES * RANK, 2 * COLS), f32)
    point_buf = pltpu.VMEM(points.shape, f32)
    skel_buf = pltpu.VMEM(skeletons.shape, f32)
    dma = pltpu.SemaphoreType.DMA
    hd, gap, scalars = pl.pallas_call(
        step_kernel,
        out_shape=(wide, wide, jax.ShapeDtypeStruct((COLS, 128), f32)),
        in_specs=[sm] + [hbm] * 10,
        out_specs=(hbm, hbm, vm),
        scratch_shapes=[
            big, big, big,
            pltpu.VMEM(device_basis.shape, f32),
            pltpu.VMEM(node_coords.shape, f32),
            point_buf, skel_buf,
            big, big, point_buf, skel_buf, weights, weights,
            pltpu.VMEM((9, 64, 128), f32),
            pltpu.VMEM((6, 128, 128), f32),
            pltpu.VMEM((4, 4, 64, 128), f32),
            pltpu.VMEM((6, 128, 128), f32),
            pltpu.VMEM((64, 128), f32),
            pltpu.VMEM((65, 256, 256), bf16),
            pltpu.VMEM((65, 256, 64), bf16),
            pltpu.VMEM((32, 64, 256), bf16),
            pltpu.VMEM((65, 64, 256), bf16),
            pltpu.VMEM((65, 64, 128), bf16),
            pltpu.VMEM((65, 64, 128), bf16),
            pltpu.VMEM((32, 64, 64), bf16),
            pltpu.VMEM((32, 64, 128), f32),
            pltpu.VMEM((32, 128, 128), bf16),
            pltpu.VMEM((STEPS * BUFS + 1, 128, 256), f32),
            pltpu.VMEM((BUFS, 256, 256), bf16),
            pltpu.VMEM((BUFS, 256, 256), bf16),
            pltpu.VMEM((4, 64, 128), f32),
            pltpu.VMEM((4, 4, 8, 128), f32),
            dma((5 + 3 * CHUNKS,)), dma((6,)), dma((5,)), dma((5,)),
            dma((4, 3)), dma((4, 3)), dma((4, 3)), dma((4, 3)), dma((2,)), dma((2,)),
        ],
        compiler_params=pltpu.CompilerParams(
            collective_id=0, has_side_effects=True, vmem_limit_bytes=VMEM_LIMIT
        ),
    )(
        lists(near_list, far_list), direction, iterate, leaf_basis, device_basis, transfer,
        node_coords, points, skeletons, residual, rhs,
    )
    block = pl.BlockSpec((COLS, UPDATE), lambda i: (0, i))
    return pl.pallas_call(
        update_kernel,
        grid=(LEAVES * LEAF // UPDATE,),
        out_shape=(wide,) * 4,
        in_specs=[pl.BlockSpec((COLS, 128), lambda i: (0, 0))] + [block] * 5,
        out_specs=(block,) * 4,
        compiler_params=pltpu.CompilerParams(vmem_limit_bytes=VMEM_LIMIT),
    )(scalars, iterate, direction, residual, hd, gap)


def solution(mesh):
    wide = P(None, ("leaf", "sub"))
    rows = P(("leaf", "sub"), None)
    return jax.shard_map(
        shards,
        mesh=mesh,
        in_specs=(wide,) * 8 + (P(), P(), rows, rows),
        out_specs=(wide,) * 4,
        check_vma=False,
    )
```

```python
import functools
import math

import jax
import jax.numpy as jnp
from jax import lax
from jax.experimental import pallas as pl
from jax.experimental.pallas import tpu as pltpu
from jax.sharding import PartitionSpec as P

MESH = pl.DeviceIdType.MESH
f32, bf16 = jnp.float32, jnp.bfloat16
noise_level = 1.0
amplitude = 0.1
length_scale = 1.0
LN2 = math.log(2.0)
COORD = math.sqrt(3.0) / length_scale / LN2
LEAVES, LEAF, RANK, COLS = 32, 256, 64, 64
SLOTS, BUFS, AHEAD = 200, 8, 4
STEPS, CHUNKS = 24, 4
RING_AT, DOWN_AT = (5, 9, 13), 17
ALONE, UPDATE = 3, 16
VMEM_LIMIT = 63 << 20
CORE = (1,)
RINGS = ((2, 4, 6), (8, 16, 24), (32, 64, 96))
SUM_ROUNDS = (tuple(range(1, 8)), tuple(range(8, 128, 8)))


def dot(a, b):
    return lax.dot_general(a, b, (((1,), (0,)), ((), ())), preferred_element_type=f32)


def dot_nt(a, b):
    return lax.dot_general(a, b, (((1,), (1,)), ((), ())), preferred_element_type=f32)


def split(a):
    hi = a.astype(bf16)
    return hi, (a - hi.astype(f32)).astype(bf16)


def dot3(a, b):
    ah, al = split(a)
    bh, bl = split(b)
    return dot(ah, bh) + (dot(ah, bl) + dot(al, bh))


def kern(u):
    t = jnp.maximum(u, 1e-12)
    s = t * lax.rsqrt(t)
    return (amplitude + (amplitude * LN2) * s) * jnp.exp2(-s)


def pieces(a):
    one = a.astype(bf16).astype(f32)
    rest = a - one
    two = rest.astype(bf16).astype(f32)
    three = (rest - two).astype(bf16).astype(f32)
    return one, two, three


def features(coords):
    a = coords * COORD
    a1, a2, a3 = pieces(a)
    n1, n2, n3 = pieces(jnp.sum(a * a, axis=0, keepdims=True))
    row = lax.broadcasted_iota(jnp.int32, a.shape, 0)
    norm = jnp.where((row == 0) | (row == 3), n1, jnp.where((row == 1) | (row == 4), n2, n3))
    zero = jnp.zeros_like(a)
    src_norm = jnp.where(row < 3, norm, jnp.where(row < 6, 1.0, 0.0))
    tgt_norm = jnp.where(row < 3, 1.0, jnp.where(row < 6, norm, 0.0))
    s1, s2, s3 = -2.0 * a1, -2.0 * a2, -2.0 * a3
    source = jnp.concatenate([s1, s1, s2, s2, s1, s3, src_norm, zero], axis=0)
    target = jnp.concatenate([a1, a2, a1, a2, a3, a1, tgt_norm, zero], axis=0)
    return source, target


def tree_position():
    return lax.axis_index("sub") * 32 + lax.axis_index("leaf")


def device_at(q):
    return (lax.rem(q, 32), lax.div(q, 32))


def greet(masks):
    q = tree_position()
    barrier = pltpu.get_barrier_semaphore()
    for mask in masks:
        pl.semaphore_signal(barrier, inc=1, device_id=device_at(q ^ mask), device_id_type=MESH)


def await_greetings(masks):
    pl.semaphore_wait(pltpu.get_barrier_semaphore(), len(masks))


def exchange(buf, number, masks, send, recv):
    q = tree_position()
    return [
        pltpu.make_async_remote_copy(
            buf.at[number, 0],
            buf.at[number, i + 1],
            send.at[number, i],
            recv.at[number, i],
            device_id=device_at(q ^ mask),
            device_id_type=MESH,
        )
        for i, mask in enumerate(masks)
    ]


def lists(near_in, far_in, flat_v, pairs_v, rows_v, pairs, rows_s, sems):
    shape = (LEAVES, 256)
    leaf = lax.broadcasted_iota(jnp.int32, shape, 0)
    slot = lax.broadcasted_iota(jnp.int32, shape, 1)
    tall = []
    for i, ref in enumerate((near_in, far_in)):
        flat_v[i] = jnp.full((8, 128), -1, jnp.int32)
        flat_v[i, :, :LEAVES] = ref[...]
        tall.append(flat_v[i].T[:LEAVES])
    near, far = tall
    entry = [jnp.broadcast_to(near[:, j : j + 1], shape) for j in range(8)]
    others = jnp.zeros(shape, jnp.int32)
    for j in range(1, 8):
        others = others + jnp.where(entry[j] >= 0, 1, 0)
    upto = others
    for step in (1, 2, 4, 8, 16):
        upto = upto + jnp.where(leaf >= step, pltpu.roll(upto, step, 0), 0)
    before = upto - others + LEAVES
    nothing = 64 + 31 * 128 + 4096
    total = jnp.zeros(shape, jnp.int32)
    for j in range(8):
        place = leaf if j == 0 else before + (j - 1)
        code = entry[j] + leaf * 128 + ((0 if j < 2 else 4096) - nothing)
        total = total + jnp.where((place == slot) & (entry[j] >= 0), code, 0)
    for step in (16, 8, 4, 2, 1):
        total = total + pltpu.roll(total, step, 0)
    pairs_v[...] = total[:8] + nothing
    ends = jnp.where(others > 0, jnp.minimum(before + others, STEPS * BUFS), 0)
    rows_v[...] = ends[:, :128]
    rows_v[:, :8] = jnp.where(far < 0, 64, far)
    copies = [
        pltpu.make_async_copy(pairs_v, pairs, sems.at[0]),
        pltpu.make_async_copy(rows_v, rows_s, sems.at[1]),
    ]
    for copy in copies:
        copy.start()
    return copies


def step_kernel(
    near_in, far_in, d_in, x_in, lb_in, db_in, transfer, nc_in, pts_in, sk_in, res_in, rhs_in,
    hd_out, gap_out, scalars,
    d, x, lb, db, nc, pts, sk, dp, xp, ptp, skp, w_own, wp,
    mats, kmask, buf, stk, z0, vt, fs, ft, wt, fte, fto, fsk, zl, zt, terms, kh, kl, tot, abuf,
    in_sem, mat_sem, far_send, far_recv, send, recv, asend, arecv, out_sem, late_sem,
    flat_v, pairs_v, rows_v, pairs, rows_s, list_sem,
):
    q = tree_position()
    every = sum(SUM_ROUNDS, ())
    greet(every)
    list_copies = lists(near_in, far_in, flat_v, pairs_v, rows_v, pairs, rows_s, list_sem)
    chunk = LEAVES * LEAF // CHUNKS
    loads = [
        pltpu.make_async_copy(a, b, in_sem.at[i])
        for i, (a, b) in enumerate(((pts_in, pts), (sk_in, sk), (nc_in, nc), (db_in, db)))
    ]
    for load in loads[:1]:
        load.start()
    parts = []
    for c in range(CHUNKS):
        at = pl.ds(c * chunk, chunk)
        parts.append([
            pltpu.make_async_copy(a.at[:, at], b.at[:, at], in_sem.at[5 + 3 * c + i])
            for i, (a, b) in enumerate(((d_in, d), (x_in, x), (lb_in, lb)))
        ])
        for load in parts[-1]:
            load.start()
        if c == 0:
            for load in loads[1:]:
                load.start()
    spots = []
    for c in range(1, 7):
        base = 128 - 2 * (128 >> c)
        node = lax.shift_right_logical(q, c)
        if c % 2:
            spots.append((base + node, 1, (c - 1) // 2 * 3))
        else:
            spots.append((base + (node & -2), 2, (c - 2) // 2 * 3 + 1))
    mat_loads = [
        pltpu.make_async_copy(transfer.at[pl.ds(at, n)], mats.at[pl.ds(slot, n)], mat_sem.at[i])
        for i, (at, n, slot) in enumerate(spots)
    ]
    for load in mat_loads:
        load.start()

    def lanes(l, width):
        return pl.ds(pl.multiple_of(l * width, width), width)

    await_greetings(every)
    partner = device_at(q ^ 1)
    bulk = [
        pltpu.make_async_remote_copy(
            a, b, far_send.at[i], far_recv.at[i], device_id=partner, device_id_type=MESH
        )
        for i, (a, b) in enumerate(
            ((pts_in, ptp), (d_in, dp), (x_in, xp), (sk_in, skp), (w_own, wp))
        )
    ]
    for copy in bulk[:4]:
        copy.start()

    loads[0].wait()

    def own_points(l, carry):
        source, target = features(pts[:, lanes(l, LEAF)])
        fs[l] = source.T.astype(bf16)
        ft[l] = target.astype(bf16)
        return carry

    lax.fori_loop(0, LEAVES, own_points, 0, unroll=4)

    def leaf(l, carry):
        at = lanes(l, LEAF)
        vh, vl = split(jnp.concatenate([d[:, at], x[:, at]], axis=0))
        vt[l] = jnp.concatenate([vh, vl], axis=0)
        bh, bl = split(lb[:, at])
        both = dot_nt(jnp.concatenate([bh, bl], axis=0), vh)
        w_own[lanes(l, RANK), :] = both[:RANK] + both[RANK:] + dot_nt(bh, vl)
        return carry

    for c in range(CHUNKS):
        for load in parts[c]:
            load.wait()
        lax.fori_loop(c * LEAVES // CHUNKS, (c + 1) * LEAVES // CHUNKS, leaf, 0, unroll=4)
    bulk[4].start()
    for load in loads[1:]:
        load.wait()
    buf[0, 0] = dot3(db[...], w_own[...])
    for copy in exchange(buf, 0, CORE, send, recv):
        copy.start()

    row = lax.broadcasted_iota(jnp.int32, (128, 128), 0)
    col = lax.broadcasted_iota(jnp.int32, (128, 128), 1)
    for c in range(1, 7):
        start = 64 * (128 - 2 * (128 >> c)) + 128 * lax.shift_right_logical(q, c + 1)
        source, target = features(nc[:, pl.ds(pl.multiple_of(start, 128), 128)])
        full = kern(dot(source.T.astype(bf16), target.astype(bf16)))
        kmask[c - 1] = jnp.where((row < 64) == (col < 64), 0.0, full)
    for load in mat_loads:
        load.wait()

    def skel_tables(side, ss, ww):
        low = lax.broadcasted_iota(jnp.int32, (64, 128), 1) < 64

        def one_pair(m, carry):
            source, target = features(ss[:, lanes(m, 128)])
            turned = pltpu.roll(target, 64, 1)
            one = side * LEAVES + 2 * m
            fte[one] = jnp.where(low, target, 0.0).astype(bf16)
            fto[one] = jnp.where(low, 0.0, turned).astype(bf16)
            fte[one + 1] = jnp.where(low, turned, 0.0).astype(bf16)
            fto[one + 1] = jnp.where(low, 0.0, target).astype(bf16)
            for i in range(2):
                hi, lo = split(ww[pl.ds(pl.multiple_of(m * 128 + i * 64, 64), 64), :])
                wt[one + i] = jnp.concatenate([hi, lo], axis=1)
            if side == 0:
                flipped = source.T.astype(bf16)
                fsk[2 * m] = flipped[:64]
                fsk[2 * m + 1] = flipped[64:]
            return carry

        lax.fori_loop(0, LEAVES // 2, one_pair, 0, unroll=4)

    skel_tables(0, sk, w_own)
    vt[2 * LEAVES] = jnp.zeros((4 * COLS, LEAF), bf16)
    fs[2 * LEAVES] = jnp.zeros((LEAF, 64), bf16)
    wt[2 * LEAVES] = jnp.zeros((RANK, 4 * COLS), bf16)
    fte[2 * LEAVES] = jnp.zeros((64, 128), bf16)
    fto[2 * LEAVES] = jnp.zeros((64, 128), bf16)
    terms[0] = jnp.zeros((2 * COLS, LEAF), f32)
    zero = jnp.zeros((COLS, 128), f32)
    for i in range(4):
        tot[i] = zero

    def pair(number, a, b):
        return jnp.concatenate([buf[number, a ^ (2 * b)], buf[number, a ^ (2 * b + 1)]], axis=0)

    def half(value, c):
        return jnp.where((lax.shift_right_logical(q, c) & 1) == 0, value[:64], value[64:])

    def climb_core():
        for copy in exchange(buf, 0, CORE, send, recv):
            copy.wait()
        h = q & 1
        bottom = jnp.concatenate([buf[0, h], buf[0, h ^ 1]], axis=0)
        buf[1, 0] = dot3(mats[0], bottom)
        for copy in exchange(buf, 1, RINGS[0], send, recv):
            copy.start()

    def climb_ring(r):
        for copy in exchange(buf, r + 1, RINGS[r], send, recv):
            copy.wait()
        a = lax.shift_right_logical(q, 2 * r + 1) & 3
        e = a & 2
        stk[2 * r] = jnp.concatenate([buf[r + 1, a ^ e], buf[r + 1, a ^ (e + 1)]], axis=0)
        upper = jnp.concatenate(
            [dot3(mats[3 * r + 1 + b], pair(r + 1, a, b)) for b in range(2)], axis=0
        )
        stk[2 * r + 1] = upper
        if r < 2:
            buf[r + 2, 0] = dot3(mats[3 * r + 3], upper)
            for copy in exchange(buf, r + 2, RINGS[r + 1], send, recv):
                copy.start()

    def descend():
        down = half(dot3(kmask[5], stk[5]), 6)
        for c in range(6, 0, -1):
            if c % 2:
                matrix = mats[(c - 1) // 2 * 3]
            else:
                matrix = mats[(c - 2) // 2 * 3 + 1 + (lax.shift_right_logical(q, c) & 1)]
            children = dot3(matrix.T, down)
            if c > 1:
                children = children + dot3(kmask[c - 2], stk[c - 2])
            down = half(children, c - 1)
        z0[...] = down

    def tile(k, b):
        code = pairs[0, k]
        hi, lo = split(kern(dot(fs[code & 127], ft[lax.shift_right_logical(code, 7) & 31])))
        kh[b] = hi
        kl[b] = lo

    def multiply(k, b):
        code = pairs[0, k]
        v = vt[code & 127]
        keep = lax.shift_right_logical(code, 12).astype(f32)
        both = dot(v, kh[b])
        terms[k + 1] = terms[k] * keep + (
            both[: 2 * COLS] + both[2 * COLS :] + dot(v[: 2 * COLS], kl[b])
        )

    for copy in list_copies:
        copy.wait()
    for j in range(AHEAD):
        tile(j, j)

    def near_step(i):
        for j in range(BUFS):
            k = i * BUFS + j
            multiply(k, j)
            tile(k + AHEAD, (j + AHEAD) % BUFS)

    def near_alone(i, carry):
        near_step(i)
        return carry

    lax.fori_loop(0, ALONE, near_alone, 0)
    climb_core()

    for copy in bulk[:3]:
        copy.wait()

    def partner_points(l, carry):
        at = lanes(l, LEAF)
        source, target = features(ptp[:, at])
        fs[LEAVES + l] = source.T.astype(bf16)
        hi, lo = split(jnp.concatenate([dp[:, at], xp[:, at]], axis=0))
        vt[LEAVES + l] = jnp.concatenate([hi, lo], axis=0)
        return carry

    lax.fori_loop(0, LEAVES, partner_points, 0, unroll=4)
    late = [
        pltpu.make_async_copy(a, b, late_sem.at[i])
        for i, (a, b) in enumerate(((res_in, dp), (rhs_in, xp)))
    ]
    for load in late:
        load.start()

    def near(i, carry):
        for r in range(3):
            @pl.when(i == RING_AT[r])
            def _():
                climb_ring(r)

        @pl.when(i == DOWN_AT)
        def _():
            descend()

        near_step(i)
        return carry

    lax.fori_loop(ALONE, STEPS, near, 0)

    for copy in bulk[3:]:
        copy.wait()
    skel_tables(1, skp, wp)

    def down_to_leaves(m, carry):
        dh, dl = split(db[:, lanes(m, 128)].T)
        zh, zlo = split(z0[...])
        part = dot(dh, zh) + (dot(dh, zlo) + dot(dl, zh))
        zl[2 * m] = part[:64]
        zl[2 * m + 1] = part[64:]
        return carry

    lax.fori_loop(0, LEAVES // 2, down_to_leaves, 0, unroll=4)

    def farther(l, carry):
        across = []
        rows = []
        for j in range(4):
            one, two = rows_s[l, 2 * j], rows_s[l, 2 * j + 1]
            across.append(fte[one] + fto[two])
            rows += [wt[one], wt[two]]
        hi, lo = split(kern(dot(fsk[l], jnp.concatenate(across, axis=1))))
        got = dot(jnp.concatenate([hi, lo], axis=0), jnp.concatenate(rows, axis=0))
        zl[l] += got[:64, :128] + got[:64, 128:] + got[64:, :128]
        return carry

    lax.fori_loop(0, LEAVES, farther, 0, unroll=4)

    def turn(l, carry):
        z = zl[l]
        zh = z.astype(bf16).astype(f32)
        zt[l] = jnp.concatenate([zh, z - zh], axis=0).T.astype(bf16)
        return carry

    lax.fori_loop(0, LEAVES, turn, 0, unroll=8)
    for load in late:
        load.wait()

    def fold(value):
        return value[:, :128] + value[:, 128:]

    def applied(l, at, rows):
        bh, bl = split(lb[:, at])
        zz = zt[l, rows]
        pairs = terms[1 + l, rows] + terms[rows_s[l, 8], rows]
        return pairs + (dot(zz, jnp.concatenate([bh, bh], axis=0)) + dot(zz[:, :64], bl))

    def finish(l, carry):
        at = lanes(l, LEAF)
        dl = d[:, at]
        r = dp[:, at]
        image = noise_level * dl + applied(l, at, pl.ds(0, COLS))
        tot[0] += fold(dl * image)
        tot[1] += fold(r * image)
        tot[2] += fold(image * image)
        tot[3] += fold(r * r)
        d[:, at] = image
        return carry

    def finish_iterate(l, carry):
        at = lanes(l, LEAF)
        x[:, at] = xp[:, at] - (noise_level * x[:, at] + applied(l, at, pl.ds(COLS, COLS)))
        return carry

    lax.fori_loop(0, LEAVES, finish, 0, unroll=4)
    outs = [
        pltpu.make_async_copy(a, b, out_sem.at[i])
        for i, (a, b) in enumerate(((d, hd_out), (x, gap_out)))
    ]
    outs[0].start()

    lane = lax.broadcasted_iota(jnp.int32, (COLS, 128), 1)
    packed = zero
    for i in range(4):
        packed = jnp.where(lane == i, jnp.sum(tot[i], axis=1, keepdims=True), packed)
    value = jnp.concatenate([packed, zero], axis=0).T[:8]
    for r, masks in enumerate(SUM_ROUNDS):
        abuf[r, 0] = value
        copies = exchange(abuf, r, masks, asend, arecv)
        for copy in copies:
            copy.start()
        if r == 0:
            lax.fori_loop(0, LEAVES, finish_iterate, 0, unroll=4)
            outs[1].start()
        for copy in copies:
            copy.wait()
        value = jnp.sum(abuf[r, : len(masks) + 1], axis=0)
    curv, cross, square, old = value[0:1], value[1:2], value[2:3], value[3:4]
    alpha = old / curv
    new = old - 2.0 * alpha * cross + alpha * alpha * square
    beta = new / old
    eight = lax.broadcasted_iota(jnp.int32, (8, 128), 0)
    value = jnp.where(eight == 0, alpha, jnp.where(eight == 1, beta, 0.0))
    scalars[...] = jnp.concatenate([value, jnp.zeros((120, 128), f32)], axis=0).T[:COLS]
    for out in outs:
        out.wait()


def update_kernel(scalars, it, d, r, hd, gap, new_it, new_r, new_d, true_r):
    alpha, beta = scalars[:, 0:1], scalars[:, 1:2]
    dd, step = d[...], alpha * hd[...]
    rr = r[...] - step
    new_it[...] = it[...] + alpha * dd
    new_r[...] = rr
    new_d[...] = rr + beta * dd
    true_r[...] = gap[...] - step


def shards(
    rhs, iterate, residual, direction, points, skeletons, leaf_basis, device_basis, transfer,
    node_coords, near_list, far_list,
):
    vm = pl.BlockSpec(memory_space=pltpu.VMEM)
    hbm = pl.BlockSpec(memory_space=pl.ANY)
    wide = jax.ShapeDtypeStruct((COLS, LEAVES * LEAF), f32)
    big = pltpu.VMEM((COLS, LEAVES * LEAF), f32)
    weights = pltpu.VMEM((LEAVES * RANK, 2 * COLS), f32)
    point_buf = pltpu.VMEM(points.shape, f32)
    skel_buf = pltpu.VMEM(skeletons.shape, f32)
    dma = pltpu.SemaphoreType.DMA
    hd, gap, scalars = pl.pallas_call(
        step_kernel,
        out_shape=(wide, wide, jax.ShapeDtypeStruct((COLS, 128), f32)),
        in_specs=[vm] * 2 + [hbm] * 10,
        out_specs=(hbm, hbm, vm),
        scratch_shapes=[
            big, big, big,
            pltpu.VMEM(device_basis.shape, f32),
            pltpu.VMEM(node_coords.shape, f32),
            point_buf, skel_buf,
            big, big, point_buf, skel_buf, weights, weights,
            pltpu.VMEM((9, 64, 128), f32),
            pltpu.VMEM((6, 128, 128), f32),
            pltpu.VMEM((4, 4, 64, 128), f32),
            pltpu.VMEM((6, 128, 128), f32),
            pltpu.VMEM((64, 128), f32),
            pltpu.VMEM((65, 256, 256), bf16),
            pltpu.VMEM((65, 256, 64), bf16),
            pltpu.VMEM((32, 64, 256), bf16),
            pltpu.VMEM((65, 64, 256), bf16),
            pltpu.VMEM((65, 64, 128), bf16),
            pltpu.VMEM((65, 64, 128), bf16),
            pltpu.VMEM((32, 64, 64), bf16),
            pltpu.VMEM((32, 64, 128), f32),
            pltpu.VMEM((32, 128, 128), bf16),
            pltpu.VMEM((STEPS * BUFS + 1, 128, 256), f32),
            pltpu.VMEM((BUFS, 256, 256), bf16),
            pltpu.VMEM((BUFS, 256, 256), bf16),
            pltpu.VMEM((4, 64, 128), f32),
            pltpu.VMEM((2, 16, 8, 128), f32),
            dma((5 + 3 * CHUNKS,)), dma((6,)), dma((5,)), dma((5,)),
            dma((4, 3)), dma((4, 3)), dma((2, 15)), dma((2, 15)), dma((2,)), dma((2,)),
            pltpu.VMEM((2, 8, 128), jnp.int32),
            pltpu.VMEM((8, 256), jnp.int32),
            pltpu.VMEM((LEAVES, 128), jnp.int32),
            pltpu.SMEM((8, 256), jnp.int32),
            pltpu.SMEM((LEAVES, 128), jnp.int32),
            dma((2,)),
        ],
        compiler_params=pltpu.CompilerParams(
            collective_id=0, has_side_effects=True, vmem_limit_bytes=VMEM_LIMIT
        ),
    )(
        near_list.T, far_list.T, direction, iterate, leaf_basis, device_basis, transfer,
        node_coords, points, skeletons, residual, rhs,
    )
    block = pl.BlockSpec((UPDATE, LEAVES * LEAF), lambda i: (i, 0))
    return pl.pallas_call(
        update_kernel,
        grid=(COLS // UPDATE,),
        out_shape=(wide,) * 4,
        in_specs=[pl.BlockSpec((UPDATE, 128), lambda i: (i, 0))] + [block] * 5,
        out_specs=(block,) * 4,
        compiler_params=pltpu.CompilerParams(vmem_limit_bytes=VMEM_LIMIT),
    )(scalars, iterate, direction, residual, hd, gap)


def solution(mesh):
    wide = P(None, ("leaf", "sub"))
    rows = P(("leaf", "sub"), None)
    return jax.shard_map(
        shards,
        mesh=mesh,
        in_specs=(wide,) * 8 + (P(), P(), rows, rows),
        out_specs=(wide,) * 4,
        check_vma=False,
    )
```
